256 devices in a mesh: group: 8 (over z), member: 32 (over x, y, core).
Axes of the slice: x: 4, y: 4, z: 8, core: 2. Of those that a mesh axis runs over, the one named last changes fastest.
Arguments:
- packed_words: int32 [28672, 32, 256], P(('group', 'member')), may hold values from 0 to 4095
- bit_widths: int32 [28672, 256], P(('group', 'member')), may hold values from 1 to 3
- column_bases: int32 [28672, 256], P(('group', 'member')), may hold values from -20 to 20
- column_scale: float32 [256], replicated, may hold values from 0.01 to 0.1
- block_owner: int32 [28672, 1], P(('group', 'member')), may hold values from 0 to 31; in each aligned block of 112 rows (0 to 111, 112 to 223, ...) at most 14 rows name the same one
- block_key: int32 [28672], P(('group', 'member')), may hold values from 0 to 255
- predicate_bounds: int32 [4], replicated, may hold values from -20 to 27
Outputs:
- key_means: float32 [8192, 256], P(('group', 'member'))
- key_mean_squares: float32 [8192, 256], P(('group', 'member'))
- row_share: float32 [8192], P(('group', 'member'))
The draws below stay inside these ranges and needn't reach their ends.
Inputs may be any that keep to these rules, and one draw needn't show every extreme that they name: `block_owner`: among the blocks of one device at most 14 name the same owner, and some device's blocks name one owner exactly 14 times.
All inputs are finite; a program needn't handle non-finite values.
Results may differ from the reference program's by a relative error of at most 0.0003.
Values sent between devices are 32-bit elements; how exact they have to be, the bound alone decides.
A program may use at most 64 MiB of HBM per device.

```python
import math
import jax
import jax.numpy as jnp
import numpy as np
from jax import lax

COLS = 256
BLOCK = 128
WORDS = 32
BLOCKS_DEV = 112
KD = 32
CAP = 14
BLOCKS = 28672
KEYS = 8192
N_GROUP = 8
N_MEMBER = 32


def draw_predicate_bounds(key, part):
    pieces = jax.random.split(key, 4)
    low_pick = jax.random.randint(pieces[0], (), 0, 2)
    high_pick = jax.random.randint(pieces[1], (), 0, 2)
    low_other = jax.random.randint(pieces[2], (), -20, 1)
    high_other = jax.random.randint(pieces[3], (), 4, 28)
    time_low = jnp.where(low_pick == 0, -20, low_other)
    value_low = jnp.where(low_pick == 0, low_other, -20)
    time_high = jnp.where(high_pick == 0, 27, high_other)
    value_high = jnp.where(high_pick == 0, high_other, 27)
    return jnp.stack([time_low, time_high, value_low, value_high]).astype(jnp.int32)


def plant(drawn, stream_key, low, high):
    longest = drawn.shape.index(max(drawn.shape))
    spots = []
    for shift in (0, 1):
        where = [jax.random.randint(jax.random.fold_in(stream_key, axis), (), 0, length) for axis, length in enumerate(drawn.shape)]
        where[longest] = (where[longest] + shift) % drawn.shape[longest]
        spots.append(tuple(where))
    return drawn.at[spots[0]].set(low).at[spots[1]].set(high)


def cumulative_ranks(number_of, skew):
    weights = [(1 << 20) // math.isqrt(grade ** skew) + 1 for grade in range(1, number_of + 1)]
    width = 1 + sum(weights) // (1 << 30)
    return np.cumsum(np.array([max(1, weight // width) for weight in weights]))


def ranked_ids(stream_key, shape, amount, skew):
    table = cumulative_ranks(amount, skew)
    ticket = jax.random.randint(jax.random.fold_in(stream_key, 1), shape, 0, int(table[amount - 1]))
    standing = jnp.searchsorted(jnp.asarray(table, jnp.int32), ticket, side="right")
    return jax.random.permutation(jax.random.fold_in(stream_key, 2), amount)[standing].astype(jnp.int32)


def deal_out(stream_key, own, number, rows, count, top, bound, lean):
    order = jax.random.permutation(stream_key, count)
    heavy_load, ordinary = portions_of(count, rows * top, bound, lean, True), portions_of(count, rows * top, bound, lean, False)
    places = jnp.arange(count)

    def named(lengths, rotation):
        used = int((lengths > 0).sum())
        fixed = max(1, used // 4)
        passed = fixed + (places - fixed + rotation * (used - fixed)) % max(1, count - fixed)
        return jnp.zeros((count,), jnp.int32).at[order[jnp.where(places < fixed, places, passed)]].set(jnp.asarray(lengths, jnp.int32))

    lengths = jnp.where(number % 4 == 0, named(heavy_load, number // 4), named(ordinary, number - number // 4 - 1))
    mixed = jax.random.permutation(jax.random.fold_in(own, 3), count)
    giver, sink = mixed[0:count // 2 * 2:2], mixed[1:count // 2 * 2:2]
    margin = jnp.minimum(lengths[giver] - 1, bound - lengths[sink]) // 2
    margin = jnp.where((giver == order[0]) | (sink == order[0]) | (lengths[sink] == 0), 0, jnp.maximum(margin, 0))
    passed = jax.random.randint(jax.random.fold_in(own, 4), (count // 2,), 0, 1 << 20) % (margin + 1)
    lengths = lengths.at[giver].add(-passed).at[sink].add(passed)
    labels = jnp.searchsorted(jnp.cumsum(lengths), jnp.arange(rows * top), side="right").astype(jnp.int32)
    grid = labels.reshape(top, rows).T
    grid = grid[jax.random.permutation(jax.random.fold_in(own, 1), rows)]
    rotation = jax.random.randint(jax.random.fold_in(own, 2), (rows, 1), 0, top)
    return jnp.take_along_axis(grid, (jnp.arange(top)[None, :] + rotation) % top, axis=1)


def portions_of(number_of, total, limit, lean, full):
    portions = [(1 << 20) // math.isqrt(rank ** lean) + 1 for rank in range(1, number_of + 1)]
    largest = limit if full else min(limit, max(-(-total // number_of), total * portions[0] // sum(portions)))
    least = 1 if total - largest >= number_of - 1 else 0
    given, rest = [largest] + [least] * (number_of - 1), total - largest - least * (number_of - 1)
    while rest > 0:
        candidates = [i for i in range(1, number_of) if given[i] < largest] or [i for i in range(1, number_of) if given[i] < limit]
        mass, left = sum([portions[i] for i in candidates]), rest
        for i in candidates:
            more = min(limit - given[i], max(1, left * portions[i] // mass), rest)
            given[i] = given[i] + more
            rest = rest - more
    return np.array(given)


def setup_inputs(seed: int = 0) -> dict:
    keys = jax.random.split(jax.random.key(seed), 8)
    packed_words = plant(jax.random.randint(keys[0], (BLOCKS, WORDS, COLS), 0, 4096), jax.random.fold_in(keys[0], 1), 0, 4095).astype(jnp.int32)
    bit_widths = plant(jax.random.randint(keys[1], (BLOCKS, COLS), 1, 4), jax.random.fold_in(keys[1], 1), 1, 3).astype(jnp.int32)
    column_bases = plant(jax.random.randint(keys[2], (BLOCKS, COLS), -20, 21), jax.random.fold_in(keys[2], 1), -20, 20).astype(jnp.int32)
    column_scale = jnp.clip(jnp.exp(jax.random.uniform(keys[3], (COLS,), jnp.float32, math.log(0.01), math.log(0.1))), 0.01, 0.1)
    block_owner_keys = jax.random.split(jax.random.fold_in(keys[4], 1), BLOCKS // BLOCKS_DEV)
    block_owner_turns = jax.random.permutation(jax.random.fold_in(keys[4], 3), BLOCKS // BLOCKS_DEV)
    block_owner = jax.vmap(lambda own, number: deal_out(jax.random.fold_in(keys[4], 2), own, number, BLOCKS_DEV, N_MEMBER, 1, CAP, 2))(block_owner_keys, block_owner_turns).reshape((BLOCKS, 1))
    block_key = plant(ranked_ids(keys[5], (BLOCKS,), N_GROUP * KD, 2), jax.random.fold_in(keys[5], 3), 0, (N_GROUP * KD) - 1).astype(jnp.int32)
    predicate_bounds = draw_predicate_bounds(jax.random.fold_in(keys[7], 71), 0)
    return dict(packed_words=packed_words, bit_widths=bit_widths, column_bases=column_bases, column_scale=column_scale, block_owner=block_owner, block_key=block_key, predicate_bounds=predicate_bounds)


def decode(packed, widths, offsets):
    result = jnp.zeros((packed.shape[0], BLOCK, packed.shape[2]), jnp.int32)
    for width_bits in (1, 2, 3):
        per_word = 12 // width_bits
        used_words = -(-BLOCK // per_word)
        shifts = jnp.arange(per_word, dtype=jnp.int32) * width_bits
        fields = jnp.right_shift(packed[:, :used_words, None, :], shifts[None, None, :, None]) & ((1 << width_bits) - 1)
        fields = fields.reshape(packed.shape[0], used_words * per_word, packed.shape[2])[:, :BLOCK, :]
        result = jnp.where((widths == width_bits)[:, None, :], fields, result)
    return result + offsets[:, None, :]


def block_stats(packed, widths, offsets, column_scale, bounds):
    decoded = decode(packed, widths, offsets)
    keep_mask = (decoded[:, :, 0] >= bounds[0]) & (decoded[:, :, 0] <= bounds[1]) & (decoded[:, :, 1] >= bounds[2]) & (decoded[:, :, 1] <= bounds[3])
    values = decoded.astype(jnp.float32) * column_scale[None, None, :]
    masked = jnp.where(keep_mask[:, :, None], values, jnp.float32(0.0))
    return jnp.sum(masked, 1), jnp.sum(masked * masked, 1), jnp.sum(keep_mask.astype(jnp.float32), 1)


def reference(packed_words, bit_widths, column_bases, column_scale, block_owner, block_key, predicate_bounds):
    total_blocks = packed_words.shape[0]
    device_count = total_blocks // BLOCKS_DEV
    columns = packed_words.shape[2]

    def per_device(pieces):
        return block_stats(pieces[0], pieces[1], pieces[2], column_scale, predicate_bounds)

    block_sums, block_squares, block_counts = lax.map(per_device, (
        packed_words.reshape(device_count, BLOCKS_DEV, WORDS, columns),
        bit_widths.reshape(device_count, BLOCKS_DEV, columns),
        column_bases.reshape(device_count, BLOCKS_DEV, columns)))
    block_sums = block_sums.reshape(total_blocks, columns)
    block_squares = block_squares.reshape(total_blocks, columns)
    block_counts = block_counts.reshape(total_blocks)
    owner_ids = block_owner[:, 0]
    global_key = (((block_key // KD) * N_MEMBER + owner_ids) * KD + block_key % KD).astype(jnp.int32)
    key_sums = jax.ops.segment_sum(block_sums, global_key, num_segments=KEYS)
    key_squares = jax.ops.segment_sum(block_squares, global_key, num_segments=KEYS)
    key_counts = jax.ops.segment_sum(block_counts, global_key, num_segments=KEYS)
    divisor = jnp.maximum(key_counts, 1.0)
    return key_sums / divisor[:, None], key_squares / divisor[:, None], key_counts / BLOCK
```

```python
import functools

import jax
import jax.numpy as jnp
from jax import lax
from jax.experimental import pallas as pl
from jax.experimental.pallas import tpu as pltpu
from jax.sharding import PartitionSpec as P

BLOCK = 128
WORDS = 32
BLOCKS_DEV = 112
KD = 32
GROUPS = 8
MEMBERS = 32
LANES = 128
SLOTS = 16
MSG = 2 * SLOTS
SENT = 30
TPITCH = 72
CHUNKS = 7
CHUNK_ROWS = 512
MESH = pl.DeviceIdType.MESH
BF16 = jnp.bfloat16
F32 = jnp.float32
I32 = jnp.int32


def iota(shape, dim):
    return lax.broadcasted_iota(I32, shape, dim)


def field_place(row):
    word3 = row >> 2
    word2 = (row * 43) >> 8
    word1 = (row * 43) >> 9
    return (word1, row - 12 * word1), (word2, row - 6 * word2), (word3, row - 4 * word3)


def spread(column):
    return jnp.broadcast_to(column, (8, LANES))


def by_width(is1, is2, one, two, three):
    return jnp.where(is1, one, jnp.where(is2, two, three))


def dot(left, right):
    return lax.dot_general(left, right, (((1,), (0,)), ((), ())), preferred_element_type=F32)


def dot_nt(left, right):
    return lax.dot_general(left, right, (((1,), (1,)), ((), ())), preferred_element_type=F32)


def split(values):
    high = values.astype(BF16)
    return high, (values - high.astype(F32)).astype(BF16)


def predicate(words, widths, bases, bounds, keep):
    lane = iota((8, LANES), 1)
    (w1, j1), (w2, j2), (w3, j3) = field_place(lane)

    def step(it, carry):
        kept = []
        for u in range(2):
            g = it * 2 + u
            width_tile = widths[pl.ds(g * 8, 8), 0:LANES]
            base_tile = bases[pl.ds(g * 8, 8), 0:LANES]
            wide, found, place = [], [], []
            for c in range(2):
                w = spread(width_tile[:, c : c + 1])
                wide.append(w)
                place.append(by_width(w == 1, w == 2, w1, w2, w3))
                found.append(jnp.zeros((8, LANES), I32))
            for j in range(WORDS):
                tile = words[0, pl.ds(g * 256 + j, 8, stride=WORDS), :]
                for c in range(2):
                    found[c] = jnp.where(place[c] == j, spread(tile[:, c : c + 1]), found[c])
            ok = None
            for c in range(2):
                w = wide[c]
                is1, is2 = w == 1, w == 2
                shift = by_width(is1, is2, j1, 2 * j2, 3 * j3)
                mask = by_width(is1, is2, 1, 3, 7)
                value = ((found[c] >> shift) & mask) + spread(base_tile[:, c : c + 1])
                inside = (value >= bounds[2 * c]) & (value <= bounds[2 * c + 1])
                ok = inside if ok is None else ok & inside
            kept.append(jnp.where(ok, 1.0, 0.0).astype(F32))
        keep[pl.ds(it * 16, 16), :] = jnp.concatenate(kept, 0).astype(BF16)
        return carry

    return step


def mask_weights():
    row, lane = iota((BLOCK, LANES), 0), iota((BLOCK, LANES), 1)
    (w1, j1), (w2, j2), (w3, j3) = field_place(row)
    pair = lane & 15
    kind = lane >> 4

    def piece(word, bits):
        return jnp.where((word & 15) == pair, jnp.where(word >= 16, bits << 12, bits), 0)

    weight = jnp.where(
        kind == 0,
        piece(w3, jnp.left_shift(7, 3 * j3)),
        jnp.where(
            kind == 1,
            piece(w2, jnp.left_shift(3, 2 * j2)),
            jnp.where(kind == 2, piece(w1, jnp.left_shift(1, j1)), jnp.where(lane == 64, 1, 0)),
        ),
    )
    return weight.astype(F32).astype(BF16)


def block_rows(words, widths, bases, masks, rows, t):
    columns = slice(t * LANES, (t + 1) * LANES)
    count = lax.population_count

    def step(it, carry):
        for u in range(2):
            g = it * 2 + u
            at = pl.ds(pl.multiple_of(g * 8, 8), 8)
            opened = masks[at, :]
            width = widths[at, columns]
            base = bases[at, columns]
            is1, is2 = width == 1, width == 2
            a0 = by_width(is1, is2, 0xFFFFFF, 0x555555, 0o11111111)
            a1 = by_width(is1, is2, 0, 0xAAAAAA, 0o22222222)
            a2 = by_width(is1, is2, 0, 0, 0o44444444)
            b01 = by_width(is1, is2, 0, 0x555555, 0o11111111)
            b02 = by_width(is1, is2, 0, 0, 0o11111111)
            b12 = by_width(is1, is2, 0, 0, 0o22222222)
            zero = jnp.zeros((8, LANES), I32)
            c0 = c1 = c2 = c01 = c02 = c12 = zero
            for i in range(16):
                low = words[t, pl.ds(g * 256 + i, 8, stride=WORDS), :]
                high = words[t, pl.ds(g * 256 + i + 16, 8, stride=WORDS), :]
                m3 = spread(opened[:, i : i + 1])
                m2 = spread(opened[:, 16 + i : 17 + i])
                m1 = spread(opened[:, 32 + i : 33 + i]) if i < 11 else zero
                m = (low | (high << 12)) & by_width(is1, is2, m1, m2, m3)
                near = m & (m >> 1)
                far = m & (m >> 2)
                c0 = c0 + count(m & a0)
                c1 = c1 + count(m & a1)
                c2 = c2 + count(m & a2)
                c01 = c01 + count(near & b01)
                c12 = c12 + count(near & b12)
                c02 = c02 + count(far & b02)
            first = c0 + 2 * c1 + 4 * c2
            second = c0 + 4 * (c1 + c01) + 8 * c02 + 16 * (c2 + c12)
            kept = spread(opened[:, 64:65])
            total = base * kept + first
            squares = base * (total + first) + second
            rows[at, 0:LANES] = total.astype(F32)
            rows[at, LANES : 2 * LANES] = squares.astype(F32)
        return carry

    return step


def kernel(
    packed, widths_in, bases_in, scale_in, owner_in, key_in, bounds_in,
    means, mean_squares, share,
    words, widths, bases, scale, owner_part, key_part, bounds,
    lanes_in, keep, masks, rows, send, recv, tsend, trecv,
    word_sems, small_sems, send_sems, recv_sems, tsend_sems, trecv_sems,
):
    group, member = lax.axis_index("group"), lax.axis_index("member")

    def word_copy(t, it):
        at = pl.ds(pl.multiple_of(it * CHUNK_ROWS, CHUNK_ROWS), CHUNK_ROWS)
        return pltpu.make_async_copy(
            packed.at[at, pl.ds(t * LANES, LANES)], words.at[t, at], word_sems.at[t, it]
        )

    small = [
        pltpu.make_async_copy(source, target, small_sems.at[i])
        for i, (source, target) in enumerate(
            [
                (bounds_in, bounds),
                (widths_in, widths),
                (bases_in, bases),
                (owner_in, owner_part),
                (key_in, key_part),
                (scale_in, scale),
            ]
        )
    ]
    for copy in small[:3]:
        copy.start()
    for t in range(2):
        for it in range(CHUNKS):
            word_copy(t, it).start()
    for copy in small[3:]:
        copy.start()

    barrier = pltpu.get_barrier_semaphore()

    def greet_member(k, carry):
        pl.semaphore_signal(
            barrier, inc=1, device_id=(group, lax.rem(member + k, MEMBERS)), device_id_type=MESH
        )
        return carry

    def greet_group(k, carry):
        pl.semaphore_signal(
            barrier, inc=1, device_id=(lax.rem(group + k, GROUPS), member), device_id_type=MESH
        )
        return carry

    for h in range(2):
        for s in range(MEMBERS):
            recv[h, s * MSG + 24 : s * MSG + 32, :] = jnp.zeros((8, LANES), F32)
    lax.fori_loop(1, MEMBERS, greet_member, 0)
    lax.fori_loop(1, GROUPS, greet_group, 0)

    small[3].wait()
    small[4].wait()
    lanes_in[...] = jnp.full((8, LANES), -1, I32)
    lanes_in[0:1, 0:BLOCKS_DEV] = owner_part[...]
    lanes_in[1:2, 0:BLOCKS_DEV] = key_part[...]
    owner = lanes_in[0:1, :]
    key = lanes_in[1:2, :]
    named = iota((MEMBERS, LANES), 0) == owner
    named_f = jnp.where(named, 1.0, 0.0).astype(F32)
    before = jnp.where(iota((LANES, LANES), 0) < iota((LANES, LANES), 1), 1.0, 0.0).astype(BF16)
    rank = jnp.sum(named_f * dot(named_f.astype(BF16), before), 0, keepdims=True).astype(I32)
    target = owner * SLOTS + rank
    placer = jnp.where(
        iota((MEMBERS * SLOTS, 2 * LANES), 0) == jnp.concatenate([target, target], 1), 1.0, 0.0
    ).astype(BF16)
    meta_lane = jnp.where(
        iota((LANES, LANES), 0) == rank + lax.rem(member, 8) * SLOTS, 1.0, 0.0
    ).astype(BF16)

    for copy in small[:3]:
        copy.wait()
    limits = [bounds[i] for i in range(4)]
    test = predicate(words, widths, bases, limits, keep)
    keep[BLOCKS_DEV:LANES, :] = jnp.zeros((LANES - BLOCKS_DEV, LANES), BF16)

    def first_pass(it, carry):
        word_copy(0, it).wait()
        return test(it, carry)

    lax.fori_loop(0, CHUNKS, first_pass, 0)
    kept = keep[...]
    masks[...] = dot(kept, mask_weights()).astype(I32)
    kept_lane = dot_nt(jnp.ones((16, LANES), BF16), kept)[0:1, :]
    meta = dot_nt(
        jnp.concatenate(
            [
                jnp.where(named, (key + 1).astype(F32), 0.0),
                jnp.where(named, jnp.broadcast_to(kept_lane, named.shape), 0.0),
            ],
            0,
        ).astype(BF16),
        meta_lane,
    )

    def message(h, other):
        return pltpu.make_async_remote_copy(
            src_ref=send.at[h, pl.ds(pl.multiple_of(other * MSG, MSG), SENT)],
            dst_ref=recv.at[h, pl.ds(pl.multiple_of(member * MSG, MSG), SENT)],
            send_sem=send_sems.at[h],
            recv_sem=recv_sems.at[h],
            device_id=(group, other),
            device_id_type=MESH,
        )

    def all_messages(h):
        at = pl.ds(0, (MEMBERS - 1) * SENT)
        return pltpu.make_async_remote_copy(
            src_ref=send.at[h, at],
            dst_ref=recv.at[h, at],
            send_sem=send_sems.at[h],
            recv_sem=recv_sems.at[h],
            device_id=(group, lax.rem(member + 1, MEMBERS)),
            device_id_type=MESH,
        )

    for h in range(2):
        work = block_rows(words, widths, bases, masks, rows, h)

        def second_pass(it, carry):
            if h == 1:
                word_copy(1, it).wait()
            return work(it, carry)

        lax.fori_loop(0, CHUNKS, second_pass, 0)
        high, low = split(rows[...])
        pad = jnp.zeros((LANES - BLOCKS_DEV, 2 * LANES), BF16)
        placed = dot(placer, jnp.concatenate([high, pad, low, pad], 0))
        for o in range(MEMBERS):
            for q in range(2):
                send[h, o * MSG + q * SLOTS : o * MSG + (q + 1) * SLOTS, :] = placed[
                    o * SLOTS : (o + 1) * SLOTS, q * LANES : (q + 1) * LANES
                ]
        if h == 0:
            send[0, pl.ds(14, MEMBERS, stride=MSG), :] = meta[0:MEMBERS, :]
            send[0, pl.ds(15, MEMBERS, stride=MSG), :] = meta[MEMBERS:, :]
            pl.semaphore_wait(barrier, MEMBERS - 1 + GROUPS - 1)

        def start_one(k, carry):
            message(h, lax.rem(member + k, MEMBERS)).start()
            return carry

        lax.fori_loop(1, MEMBERS, start_one, 0)
        own = pl.ds(pl.multiple_of(member * MSG, MSG), MSG)
        recv[h, own, :] = send[h, own, :]

    def totals_copy(h, k):
        size = 2 * KD + (8 if h == 0 else 0)
        other = lax.rem(group + k, GROUPS)
        return pltpu.make_async_remote_copy(
            src_ref=tsend.at[h, pl.ds(pl.multiple_of(other * TPITCH, 8), size)],
            dst_ref=trecv.at[h, pl.ds((k - 1) * TPITCH, size)],
            send_sem=tsend_sems.at[h, k - 1],
            recv_sem=trecv_sems.at[h, k - 1],
            device_id=(other, member),
            device_id_type=MESH,
        )

    named_key = None
    for h in range(2):
        all_messages(h).wait_recv()
        if h == 0:
            key_lanes, count_lanes = [], []
            for t in range(4):
                key_lanes.append(
                    jnp.sum(recv[0, pl.ds(t * 8 * MSG + 14, 8, stride=MSG), :], 0, keepdims=True)
                )
                count_lanes.append(
                    jnp.sum(recv[0, pl.ds(t * 8 * MSG + 15, 8, stride=MSG), :], 0, keepdims=True)
                )
            key_lane = jnp.concatenate(key_lanes, 1).astype(I32) - 1
            count_lane = jnp.concatenate(count_lanes, 1)
            width = MEMBERS * SLOTS
            named_key = jnp.where(iota((GROUPS * KD, width), 0) == key_lane, 1.0, 0.0).astype(BF16)
            by_group = jnp.where(
                iota((16, width), 0) == (key_lane >> 5), jnp.broadcast_to(count_lane, (16, width)), 0.0
            ).astype(BF16)
            in_group = jnp.where(iota((LANES, width), 0) == (key_lane & 31), 1.0, 0.0).astype(BF16)
            counts = dot_nt(by_group, in_group)
            for g in range(GROUPS):
                tsend[0, g * TPITCH + 64 : g * TPITCH + 72, :] = jnp.broadcast_to(
                    counts[g : g + 1, :], (8, LANES)
                )
        parts = [
            jnp.concatenate(
                [
                    recv[h, s * MSG + q * SLOTS : s * MSG + (q + 1) * SLOTS, :]
                    for s in range(MEMBERS)
                ],
                0,
            )
            for q in range(2)
        ]
        high, low = split(jnp.concatenate(parts, 1))
        table = dot(named_key, high) + dot(named_key, low)
        for g in range(GROUPS):
            for q in range(2):
                tsend[h, g * TPITCH + q * KD : g * TPITCH + (q + 1) * KD, :] = table[
                    g * KD : (g + 1) * KD, q * LANES : (q + 1) * LANES
                ]
        for k in range(1, GROUPS):
            totals_copy(h, k).start()

    small[5].wait()
    divisor = None
    for h in range(2):
        at = pl.multiple_of(group * TPITCH, 8)
        sums = tsend[h, pl.ds(at, KD), :]
        squares = tsend[h, pl.ds(at + KD, KD), :]
        if h == 0:
            count = tsend[0, pl.ds(at + 2 * KD, 8), :]
        for k in range(1, GROUPS):
            totals_copy(h, k).wait_recv()
            row = (k - 1) * TPITCH
            sums = sums + trecv[h, row : row + KD, :]
            squares = squares + trecv[h, row + KD : row + 2 * KD, :]
            if h == 0:
                count = count + trecv[0, row + 2 * KD : row + 2 * KD + 8, :]
        if h == 0:
            share[...] = count[0:1, 0:KD] * (1.0 / BLOCK)
            diagonal = iota((KD, LANES), 0) == iota((KD, LANES), 1)
            divisor = jnp.maximum(
                jnp.sum(
                    jnp.where(diagonal, jnp.broadcast_to(count[0:1, :], (KD, LANES)), 0.0),
                    1,
                    keepdims=True,
                ),
                1.0,
            )
        columns = slice(h * LANES, (h + 1) * LANES)
        by = scale[0:1, columns]
        means[:, columns] = sums * by / divisor
        mean_squares[:, columns] = squares * (by * by) / divisor

    for h in range(2):
        all_messages(h).wait_send()
        for k in range(1, GROUPS):
            totals_copy(h, k).wait_send()


def shards(
    packed_words, bit_widths, column_bases, column_scale, block_owner, block_key, predicate_bounds
):
    columns = packed_words.shape[2]
    hbm = pl.BlockSpec(memory_space=pltpu.HBM)
    vmem = pl.BlockSpec(memory_space=pltpu.VMEM)
    means, mean_squares, share = pl.pallas_call(
        kernel,
        out_shape=(
            jax.ShapeDtypeStruct((KD, columns), F32),
            jax.ShapeDtypeStruct((KD, columns), F32),
            jax.ShapeDtypeStruct((1, KD), F32),
        ),
        in_specs=[hbm] * 7,
        out_specs=(vmem, vmem, vmem),
        scratch_shapes=[
            pltpu.VMEM((2, BLOCKS_DEV * WORDS, LANES), I32),
            pltpu.VMEM((BLOCKS_DEV, columns), I32),
            pltpu.VMEM((BLOCKS_DEV, columns), I32),
            pltpu.VMEM((1, columns), F32),
            pltpu.VMEM((1, BLOCKS_DEV), I32),
            pltpu.VMEM((1, BLOCKS_DEV), I32),
            pltpu.SMEM((4,), I32),
            pltpu.VMEM((8, LANES), I32),
            pltpu.VMEM((LANES, LANES), BF16),
            pltpu.VMEM((LANES, LANES), I32),
            pltpu.VMEM((BLOCKS_DEV, 2 * LANES), F32),
            pltpu.VMEM((2, MEMBERS * MSG, LANES), F32),
            pltpu.VMEM((2, MEMBERS * MSG, LANES), F32),
            pltpu.VMEM((2, GROUPS * TPITCH, LANES), F32),
            pltpu.VMEM((2, (GROUPS - 1) * TPITCH, LANES), F32),
            pltpu.SemaphoreType.DMA((2, CHUNKS)),
            pltpu.SemaphoreType.DMA((6,)),
            pltpu.SemaphoreType.DMA((2,)),
            pltpu.SemaphoreType.DMA((2,)),
            pltpu.SemaphoreType.DMA((2, GROUPS - 1)),
            pltpu.SemaphoreType.DMA((2, GROUPS - 1)),
        ],
        compiler_params=pltpu.CompilerParams(
            collective_id=0, has_side_effects=True, vmem_limit_bytes=40 * 1024 * 1024
        ),
        name="rollup",
    )(
        packed_words.reshape(BLOCKS_DEV * WORDS, columns),
        bit_widths,
        column_bases,
        column_scale.reshape(1, columns),
        block_owner.reshape(1, BLOCKS_DEV),
        block_key.reshape(1, BLOCKS_DEV),
        predicate_bounds,
    )
    return means, mean_squares, share.reshape(KD)


def solution(mesh):
    return jax.shard_map(
        shards,
        mesh=mesh,
        in_specs=(
            P(("group", "member"), None, None),
            P(("group", "member"), None),
            P(("group", "member"), None),
            P(),
            P(("group", "member"), None),
            P(("group", "member")),
            P(),
        ),
        out_specs=(
            P(("group", "member"), None),
            P(("group", "member"), None),
            P(("group", "member")),
        ),
        check_vma=False,
    )
```

```python
import functools

import jax
import jax.numpy as jnp
from jax import lax
from jax.experimental import pallas as pl
from jax.experimental.pallas import tpu as pltpu
from jax.sharding import PartitionSpec as P

BLOCK = 128
WORDS = 32
BLOCKS_DEV = 112
KD = 32
GROUPS = 8
MEMBERS = 32
LANES = 128
SLOTS = 16
CAP = 14
PARTS = 4
PITCH = KD + 8
STRIDE = 13
VMEM_BYTES = 60 * 1024 * 1024
UNROLL = 7
CHUNKS = BLOCKS_DEV // (8 * UNROLL)
CHUNK_ROWS = UNROLL * 256
MESH = pl.DeviceIdType.MESH
BF16 = jnp.bfloat16
F32 = jnp.float32
I32 = jnp.int32


def iota(shape, dim):
    return lax.broadcasted_iota(I32, shape, dim)


def field_place(row):
    word3 = row >> 2
    word2 = (row * 43) >> 8
    word1 = (row * 43) >> 9
    return (word1, row - 12 * word1), (word2, row - 6 * word2), (word3, row - 4 * word3)


def spread(column):
    return jnp.broadcast_to(column, (8, LANES))


def by_width(is1, is2, one, two, three):
    return jnp.where(is1, one, jnp.where(is2, two, three))


def dot(left, right):
    return lax.dot_general(left, right, (((1,), (0,)), ((), ())), preferred_element_type=F32)


def dot_nt(left, right):
    return lax.dot_general(left, right, (((1,), (1,)), ((), ())), preferred_element_type=F32)


def split(values):
    high = values.astype(BF16)
    return high, (values - high.astype(F32)).astype(BF16)


def pick(tile, lanes):
    return jnp.take_along_axis(tile, lanes, axis=1, mode="promise_in_bounds")


def predicate(words, widths, bases, bounds, keep):
    lane = iota((8, LANES), 1)
    pair = lane >> 1
    (w1, j1), (w2, j2), (w3, j3) = field_place(lane)

    def step(it, carry):
        for u in range(UNROLL):
            g = it * UNROLL + u
            width_tile = widths[pl.ds(pl.multiple_of(g * 8, 8), 8), 0:LANES]
            base_tile = bases[pl.ds(pl.multiple_of(g * 8, 8), 8), 0:LANES]
            both = words[0, pl.ds(pl.multiple_of(g * 256, 8), 8, stride=WORDS), :]
            for j in range(1, WORDS):
                tile = words[0, pl.ds(g * 256 + j, 8, stride=WORDS), :]
                both = jnp.where(pair == j, pltpu.roll(tile, 2 * j, 1), both)
            ok = None
            for c in range(2):
                w = spread(width_tile[:, c : c + 1])
                is1, is2 = w == 1, w == 2
                word = pick(both, 2 * by_width(is1, is2, w1, w2, w3) + c)
                shift = by_width(is1, is2, j1, 2 * j2, 3 * j3)
                mask = by_width(is1, is2, 1, 3, 7)
                value = ((word >> shift) & mask) + spread(base_tile[:, c : c + 1])
                inside = (value >= bounds[2 * c]) & (value <= bounds[2 * c + 1])
                ok = inside if ok is None else ok & inside
            keep[pl.ds(pl.multiple_of(g * 8, 8), 8), :] = jnp.where(ok, 1.0, 0.0).astype(F32)
        return carry

    return step


def mask_weights():
    row, lane = iota((BLOCK, LANES), 0), iota((BLOCK, LANES), 1)
    (w1, j1), (w2, j2), (w3, j3) = field_place(row)
    pair = lane & 15
    kind = lane >> 4

    def piece(word, bits):
        return jnp.where((word & 15) == pair, jnp.where(word >= 16, bits << 12, bits), 0)

    weight = jnp.where(
        kind == 0,
        piece(w3, jnp.left_shift(7, 3 * j3)),
        jnp.where(
            kind == 1,
            piece(w2, jnp.left_shift(3, 2 * j2)),
            jnp.where(kind == 2, piece(w1, jnp.left_shift(1, j1)), jnp.where(lane == 64, 1, 0)),
        ),
    )
    return weight.astype(F32).astype(BF16)


def block_rows(words, widths, bases, masks, rows, t):
    columns = slice(t * LANES, (t + 1) * LANES)
    count = lax.population_count

    def step(it, carry):
        for u in range(UNROLL):
            g = it * UNROLL + u
            at = pl.ds(pl.multiple_of(g * 8, 8), 8)
            opened = masks[at, :]
            width = widths[at, columns]
            base = bases[at, columns]
            is1, is2 = width == 1, width == 2
            a0 = by_width(is1, is2, 0xFFFFFF, 0x555555, 0o11111111)
            a1 = jnp.where(is1, 0, a0)
            a2 = jnp.where(is1 | is2, 0, a0)
            place = by_width(is1, is2, 32, 16, 0)
            c0 = c1 = c2 = c01 = c02 = c12 = jnp.zeros((8, LANES), I32)
            for i in range(16):
                low = words[t, pl.ds(g * 256 + i, 8, stride=WORDS), :]
                high = words[t, pl.ds(g * 256 + i + 16, 8, stride=WORDS), :]
                m = (low | (high << 12)) & pick(opened, place + i)
                bit0 = m & a0
                bit1 = (m >> 1) & a1
                bit2 = (m >> 2) & a2
                c0 = c0 + count(bit0)
                c1 = c1 + count(bit1)
                c2 = c2 + count(bit2)
                c01 = c01 + count(bit0 & bit1)
                c02 = c02 + count(bit0 & bit2)
                c12 = c12 + count(bit1 & bit2)
            first = c0 + 2 * c1 + 4 * c2
            second = c0 + 4 * (c1 + c01) + 8 * c02 + 16 * (c2 + c12)
            kept = spread(opened[:, 64:65])
            total = base * kept + first
            squares = base * (total + first) + second
            rows[at, 0:LANES] = total.astype(F32)
            rows[at, LANES : 2 * LANES] = squares.astype(F32)
        return carry

    return step


def kernel(
    packed, widths_in, bases_in, scale_in, owner_in, key_in, bounds_in,
    means, mean_squares, share,
    words, widths, bases, scale, owner_part, key_part, bounds,
    lanes_in, keep, masks, rows, send, recv, tsend, trecv,
    word_sems, small_sems, send_sems, recv_sems, tsend_sems, trecv_sems,
):
    group, member = lax.axis_index("group"), lax.axis_index("member")

    def word_copy(t, it):
        at = pl.ds(pl.multiple_of(it * CHUNK_ROWS, CHUNK_ROWS), CHUNK_ROWS)
        return pltpu.make_async_copy(
            packed.at[at, pl.ds(t * LANES, LANES)], words.at[t, at], word_sems.at[t, it]
        )

    small = [
        pltpu.make_async_copy(source, target, small_sems.at[i])
        for i, (source, target) in enumerate(
            [
                (bounds_in, bounds),
                (widths_in, widths),
                (bases_in, bases),
                (owner_in, owner_part),
                (key_in, key_part),
                (scale_in, scale),
            ]
        )
    ]
    for copy in small:
        copy.start()
    for t in range(2):
        for it in range(CHUNKS):
            word_copy(t, it).start()

    for c in range(1, PARTS):
        for s in range(MEMBERS):
            recv[c, s * SLOTS + 8 : (s + 1) * SLOTS, :] = jnp.zeros((8, LANES), F32)

    barrier = pltpu.get_barrier_semaphore()

    def greet_member(k, carry):
        pl.semaphore_signal(
            barrier, inc=1, device_id=(group, lax.rem(member + k, MEMBERS)), device_id_type=MESH
        )
        return carry

    def greet_group(k, carry):
        pl.semaphore_signal(
            barrier, inc=1, device_id=(lax.rem(group + k, GROUPS), member), device_id_type=MESH
        )
        return carry

    lax.fori_loop(1, MEMBERS, greet_member, 0)
    lax.fori_loop(1, GROUPS, greet_group, 0)

    small[3].wait()
    small[4].wait()
    lanes_in[...] = jnp.full((8, LANES), -1, I32)
    lanes_in[0:1, 0:BLOCKS_DEV] = owner_part[...]
    lanes_in[1:2, 0:BLOCKS_DEV] = key_part[...]
    owner = lanes_in[0:1, :]
    key = lanes_in[1:2, :]
    named = iota((MEMBERS, LANES), 0) == owner
    named_f = jnp.where(named, 1.0, 0.0).astype(F32)
    before = jnp.where(iota((LANES, LANES), 0) < iota((LANES, LANES), 1), 1.0, 0.0).astype(BF16)
    rank = jnp.sum(named_f * dot(named_f.astype(BF16), before), 0, keepdims=True).astype(I32)
    target = owner * SLOTS + rank
    placer = jnp.where(
        iota((MEMBERS * SLOTS, 2 * LANES), 0) == jnp.concatenate([target, target], 1), 1.0, 0.0
    ).astype(BF16)
    meta_lane = jnp.where(
        iota((LANES, LANES), 0) == rank + lax.rem(member, 8) * SLOTS, 1.0, 0.0
    ).astype(BF16)
    weights = mask_weights()

    for copy in small[:3]:
        copy.wait()
    limits = [bounds[i] for i in range(4)]
    test = predicate(words, widths, bases, limits, keep)
    keep[BLOCKS_DEV:LANES, :] = jnp.zeros((LANES - BLOCKS_DEV, LANES), F32)

    def first_pass(it, carry):
        word_copy(0, it).wait()
        return test(it, carry)

    lax.fori_loop(0, CHUNKS, first_pass, 0)
    kept = keep[...].astype(BF16)
    masks[...] = dot(kept, weights).astype(I32)
    kept_lane = dot_nt(jnp.ones((16, LANES), BF16), kept)[0:1, :]
    meta = dot_nt(
        jnp.concatenate(
            [
                jnp.where(named, (key + 1).astype(F32), 0.0),
                jnp.where(named, jnp.broadcast_to(kept_lane, named.shape), 0.0),
            ],
            0,
        ).astype(BF16),
        meta_lane,
    )

    def message(c, k):
        other = lax.rem(member + k * STRIDE, MEMBERS)
        size = SLOTS if c == 0 else CAP
        return pltpu.make_async_remote_copy(
            src_ref=send.at[c, pl.ds(pl.multiple_of(other * SLOTS, SLOTS), size)],
            dst_ref=recv.at[c, pl.ds(pl.multiple_of(member * SLOTS, SLOTS), size)],
            send_sem=send_sems.at[c],
            recv_sem=recv_sems.at[c],
            device_id=(group, other),
            device_id_type=MESH,
        )

    def all_messages(c):
        at = pl.ds(0, (MEMBERS - 1) * (SLOTS if c == 0 else CAP))
        return pltpu.make_async_remote_copy(
            src_ref=send.at[c, at],
            dst_ref=recv.at[c, at],
            send_sem=send_sems.at[c],
            recv_sem=recv_sems.at[c],
            device_id=(group, lax.rem(member + 1, MEMBERS)),
            device_id_type=MESH,
        )

    def total(c, k):
        other = lax.rem(group + k, GROUPS)
        size = KD + 8 if c == 0 else KD
        return pltpu.make_async_remote_copy(
            src_ref=tsend.at[c, pl.ds(pl.multiple_of(other * PITCH, 8), size)],
            dst_ref=trecv.at[c, pl.ds(pl.multiple_of((k - 1) * PITCH, 8), size)],
            send_sem=tsend_sems.at[c],
            recv_sem=trecv_sems.at[c],
            device_id=(other, member),
            device_id_type=MESH,
        )

    def all_totals(c):
        at = pl.ds(0, (GROUPS - 1) * (KD + 8 if c == 0 else KD))
        return pltpu.make_async_remote_copy(
            src_ref=tsend.at[c, at],
            dst_ref=trecv.at[c, at],
            send_sem=tsend_sems.at[c],
            recv_sem=trecv_sems.at[c],
            device_id=(lax.rem(group + 1, GROUPS), member),
            device_id_type=MESH,
        )

    def start_messages(c):
        def start_one(k, carry):
            message(c, k).start()
            return carry

        lax.fori_loop(1, MEMBERS, start_one, 0)

    def start_totals(c, ahead):
        def start_one(k, carry):
            total(c, k).start()
            if ahead is not None:
                for i in range(4):
                    message(ahead, 4 * (k - 1) + 1 + i).start()
            return carry

        lax.fori_loop(1, GROUPS, start_one, 0)
        if ahead is not None:
            for k in range(4 * (GROUPS - 1) + 1, MEMBERS):
                message(ahead, k).start()

    for t in range(2):
        work = block_rows(words, widths, bases, masks, rows, t)

        def second_pass(it, carry):
            if t == 1:
                word_copy(1, it).wait()
            return work(it, carry)

        lax.fori_loop(0, CHUNKS, second_pass, 0)
        high, low = split(rows[...])
        pad = jnp.zeros((LANES - BLOCKS_DEV, 2 * LANES), BF16)
        placed = dot(placer, jnp.concatenate([high, pad, low, pad], 0))
        own = pl.ds(pl.multiple_of(member * SLOTS, SLOTS), SLOTS)
        for q in range(2):
            c = 2 * t + q
            send[c] = placed[:, q * LANES : (q + 1) * LANES]
            if c == 0:
                send[0, pl.ds(14, MEMBERS, stride=SLOTS), :] = meta[0:MEMBERS, :]
                send[0, pl.ds(15, MEMBERS, stride=SLOTS), :] = meta[MEMBERS:, :]
                pl.semaphore_wait(barrier, MEMBERS - 1 + GROUPS - 1)
            if t == 0:
                start_messages(c)
            recv[c, own, :] = send[c, own, :]

    named_key = None
    for c in range(PARTS):
        all_messages(c).wait_recv()
        if c == 0:
            key_lanes, count_lanes = [], []
            for b in range(4):
                for lanes, row in ((key_lanes, 14), (count_lanes, 15)):
                    tile = recv[0, pl.ds(b * 8 * SLOTS + row, 8, stride=SLOTS), :]
                    lanes.append(jnp.sum(tile, 0, keepdims=True))
            key_lane = jnp.concatenate(key_lanes, 1).astype(I32) - 1
            count_lane = jnp.concatenate(count_lanes, 1)
            width = MEMBERS * SLOTS
            named_key = jnp.where(iota((GROUPS * KD, width), 0) == key_lane, 1.0, 0.0).astype(BF16)
            by_group = jnp.where(
                iota((16, width), 0) == (key_lane >> 5), jnp.broadcast_to(count_lane, (16, width)), 0.0
            ).astype(BF16)
            in_group = jnp.where(iota((LANES, width), 0) == (key_lane & 31), 1.0, 0.0).astype(BF16)
            counts = dot_nt(by_group, in_group)
            for g in range(GROUPS):
                tsend[0, g * PITCH + KD : (g + 1) * PITCH, :] = jnp.broadcast_to(
                    counts[g : g + 1, :], (8, LANES)
                )
        high, low = split(recv[c])
        table = dot(named_key, jnp.concatenate([high, low], 1))
        table = table[:, 0:LANES] + table[:, LANES:]
        for g in range(GROUPS):
            tsend[c, g * PITCH : g * PITCH + KD, :] = table[g * KD : (g + 1) * KD, :]
        start_totals(c, c + 2 if c < 2 else None)

    small[5].wait()
    at = pl.multiple_of(group * PITCH, 8)
    divisor = None
    for c in range(PARTS):
        t, q = divmod(c, 2)
        mine = tsend[c, pl.ds(at, KD), :]
        all_totals(c).wait_recv()
        for k in range(GROUPS - 1):
            mine = mine + trecv[c, k * PITCH : k * PITCH + KD, :]
        if c == 0:
            count = tsend[0, pl.ds(at + KD, 8), :]
            for k in range(GROUPS - 1):
                count = count + trecv[0, k * PITCH + KD : (k + 1) * PITCH, :]
            share[...] = count[0:1, 0:KD] * (1.0 / BLOCK)
            diagonal = iota((KD, LANES), 0) == iota((KD, LANES), 1)
            divisor = jnp.maximum(
                jnp.sum(
                    jnp.where(diagonal, jnp.broadcast_to(count[0:1, :], (KD, LANES)), 0.0),
                    1,
                    keepdims=True,
                ),
                1.0,
            )
        columns = slice(t * LANES, (t + 1) * LANES)
        by = scale[0:1, columns]
        if q == 0:
            means[:, columns] = mine * by / divisor
        else:
            mean_squares[:, columns] = mine * (by * by) / divisor

    for c in range(PARTS):
        all_messages(c).wait_send()
        all_totals(c).wait_send()


def finish(means_in, squares_in, share_in, means, squares, share, sems):
    copies = [
        pltpu.make_async_copy(source, target, sems.at[i])
        for i, (source, target) in enumerate(
            [(means_in, means), (squares_in, squares), (share_in, share)]
        )
    ]
    for copy in copies:
        copy.start()
    for copy in copies:
        copy.wait()


def shards(
    packed_words, bit_widths, column_bases, column_scale, block_owner, block_key, predicate_bounds
):
    columns = packed_words.shape[2]
    hbm = pl.BlockSpec(memory_space=pltpu.HBM)
    vmem = pl.BlockSpec(memory_space=pltpu.VMEM)
    outs = (
        jax.ShapeDtypeStruct((KD, columns), F32),
        jax.ShapeDtypeStruct((KD, columns), F32),
        jax.ShapeDtypeStruct((1, KD), F32),
    )
    results = pl.pallas_call(
        kernel,
        out_shape=outs,
        in_specs=[hbm] * 7,
        out_specs=(vmem, vmem, vmem),
        scratch_shapes=[
            pltpu.VMEM((2, BLOCKS_DEV * WORDS, LANES), I32),
            pltpu.VMEM((BLOCKS_DEV, columns), I32),
            pltpu.VMEM((BLOCKS_DEV, columns), I32),
            pltpu.VMEM((1, columns), F32),
            pltpu.VMEM((1, BLOCKS_DEV), I32),
            pltpu.VMEM((1, BLOCKS_DEV), I32),
            pltpu.SMEM((4,), I32),
            pltpu.VMEM((8, LANES), I32),
            pltpu.VMEM((LANES, LANES), F32),
            pltpu.VMEM((LANES, LANES), I32),
            pltpu.VMEM((BLOCKS_DEV, 2 * LANES), F32),
            pltpu.VMEM((PARTS, MEMBERS * SLOTS, LANES), F32),
            pltpu.VMEM((PARTS, MEMBERS * SLOTS, LANES), F32),
            pltpu.VMEM((PARTS, GROUPS * PITCH, LANES), F32),
            pltpu.VMEM((PARTS, (GROUPS - 1) * PITCH, LANES), F32),
            pltpu.SemaphoreType.DMA((2, CHUNKS)),
            pltpu.SemaphoreType.DMA((6,)),
            pltpu.SemaphoreType.DMA((PARTS,)),
            pltpu.SemaphoreType.DMA((PARTS,)),
            pltpu.SemaphoreType.DMA((PARTS,)),
            pltpu.SemaphoreType.DMA((PARTS,)),
        ],
        compiler_params=pltpu.CompilerParams(
            collective_id=0, has_side_effects=True, vmem_limit_bytes=VMEM_BYTES
        ),
        name="rollup",
    )(
        packed_words.reshape(BLOCKS_DEV * WORDS, columns),
        bit_widths,
        column_bases,
        column_scale.reshape(1, columns),
        block_owner.reshape(1, BLOCKS_DEV),
        block_key.reshape(1, BLOCKS_DEV),
        predicate_bounds,
    )
    means, mean_squares, share = pl.pallas_call(
        finish,
        out_shape=outs,
        in_specs=[vmem] * 3,
        out_specs=(hbm, hbm, hbm),
        scratch_shapes=[pltpu.SemaphoreType.DMA((3,))],
        name="finish",
    )(*results)
    return means, mean_squares, share.reshape(KD)


def solution(mesh):
    return jax.shard_map(
        shards,
        mesh=mesh,
        in_specs=(
            P(("group", "member"), None, None),
            P(("group", "member"), None),
            P(("group", "member"), None),
            P(),
            P(("group", "member"), None),
            P(("group", "member")),
            P(),
        ),
        out_specs=(
            P(("group", "member"), None),
            P(("group", "member"), None),
            P(("group", "member")),
        ),
        check_vma=False,
    )
```

```python
import functools

import jax
import jax.numpy as jnp
from jax import lax
from jax.experimental import pallas as pl
from jax.experimental.pallas import tpu as pltpu
from jax.sharding import PartitionSpec as P

BLOCK = 128
WORDS = 32
BLOCKS_DEV = 112
KD = 32
GROUPS = 8
MEMBERS = 32
LANES = 128
SLOTS = 16
CAP = 14
PARTS = 4
PITCH = KD + 8
STRIDE = 13
VMEM_BYTES = 60 * 1024 * 1024
UNROLL = 7
CHUNKS = BLOCKS_DEV // (8 * UNROLL)
CHUNK_ROWS = UNROLL * 256
MESH = pl.DeviceIdType.MESH
BF16 = jnp.bfloat16
F32 = jnp.float32
I32 = jnp.int32


def iota(shape, dim):
    return lax.broadcasted_iota(I32, shape, dim)


def field_place(row):
    word3 = row >> 2
    word2 = (row * 43) >> 8
    word1 = (row * 43) >> 9
    return (word1, row - 12 * word1), (word2, row - 6 * word2), (word3, row - 4 * word3)


def spread(column):
    return jnp.broadcast_to(column, (8, LANES))


def by_width(is1, is2, one, two, three):
    return jnp.where(is1, one, jnp.where(is2, two, three))


def dot(left, right):
    return lax.dot_general(left, right, (((1,), (0,)), ((), ())), preferred_element_type=F32)


def dot_nt(left, right):
    return lax.dot_general(left, right, (((1,), (1,)), ((), ())), preferred_element_type=F32)


def split(values):
    high = values.astype(BF16)
    return high, (values - high.astype(F32)).astype(BF16)


def pick(tile, lanes):
    return jnp.take_along_axis(tile, lanes, axis=1, mode="promise_in_bounds")


def predicate(words, widths, bases, bounds, keep):
    lane = iota((8, LANES), 1)
    pair = lane >> 1
    (w1, j1), (w2, j2), (w3, j3) = field_place(lane)

    def step(it, carry):
        for u in range(UNROLL):
            g = it * UNROLL + u
            width_tile = widths[pl.ds(pl.multiple_of(g * 8, 8), 8), 0:LANES]
            base_tile = bases[pl.ds(pl.multiple_of(g * 8, 8), 8), 0:LANES]
            both = words[0, pl.ds(pl.multiple_of(g * 256, 8), 8, stride=WORDS), :]
            for j in range(1, WORDS):
                tile = words[0, pl.ds(g * 256 + j, 8, stride=WORDS), :]
                both = jnp.where(pair == j, pltpu.roll(tile, 2 * j, 1), both)
            ok = None
            for c in range(2):
                w = spread(width_tile[:, c : c + 1])
                is1, is2 = w == 1, w == 2
                word = pick(both, 2 * by_width(is1, is2, w1, w2, w3) + c)
                shift = by_width(is1, is2, j1, 2 * j2, 3 * j3)
                mask = by_width(is1, is2, 1, 3, 7)
                value = ((word >> shift) & mask) + spread(base_tile[:, c : c + 1])
                inside = (value >= bounds[2 * c]) & (value <= bounds[2 * c + 1])
                ok = inside if ok is None else ok & inside
            keep[pl.ds(pl.multiple_of(g * 8, 8), 8), :] = jnp.where(ok, 1.0, 0.0).astype(F32)
        return carry

    return step


def mask_weights():
    row, lane = iota((BLOCK, LANES), 0), iota((BLOCK, LANES), 1)
    (w1, j1), (w2, j2), (w3, j3) = field_place(row)
    pair = lane & 15
    kind = lane >> 4

    def piece(word, bits):
        return jnp.where((word & 15) == pair, jnp.where(word >= 16, bits << 12, bits), 0)

    weight = jnp.where(
        kind == 0,
        piece(w3, jnp.left_shift(7, 3 * j3)),
        jnp.where(
            kind == 1,
            piece(w2, jnp.left_shift(3, 2 * j2)),
            jnp.where(kind == 2, piece(w1, jnp.left_shift(1, j1)), jnp.where(lane == 64, 1, 0)),
        ),
    )
    return weight.astype(F32).astype(BF16)


def block_rows(words, widths, bases, masks, rows, t):
    columns = slice(t * LANES, (t + 1) * LANES)
    count = lax.population_count

    def step(it, carry):
        for u in range(UNROLL):
            g = it * UNROLL + u
            at = pl.ds(pl.multiple_of(g * 8, 8), 8)
            opened = masks[at, :]
            width = widths[at, columns]
            base = bases[at, columns]
            is1, is2 = width == 1, width == 2
            a0 = by_width(is1, is2, 0xFFFFFF, 0x555555, 0o11111111)
            a1 = jnp.where(is1, 0, a0)
            a2 = jnp.where(is1 | is2, 0, a0)
            place = by_width(is1, is2, 32, 16, 0)
            c0 = c1 = c2 = c01 = c02 = c12 = jnp.zeros((8, LANES), I32)
            for i in range(16):
                low = words[t, pl.ds(g * 256 + i, 8, stride=WORDS), :]
                high = words[t, pl.ds(g * 256 + i + 16, 8, stride=WORDS), :]
                m = (low | (high << 12)) & pick(opened, place + i)
                bit0 = m & a0
                bit1 = (m >> 1) & a1
                bit2 = (m >> 2) & a2
                c0 = c0 + count(bit0)
                c1 = c1 + count(bit1)
                c2 = c2 + count(bit2)
                c01 = c01 + count(bit0 & bit1)
                c02 = c02 + count(bit0 & bit2)
                c12 = c12 + count(bit1 & bit2)
            first = c0 + 2 * c1 + 4 * c2
            second = c0 + 4 * (c1 + c01) + 8 * c02 + 16 * (c2 + c12)
            kept = spread(opened[:, 64:65])
            total = base * kept + first
            squares = base * (total + first) + second
            rows[at, 0:LANES] = total.astype(F32)
            rows[at, LANES : 2 * LANES] = squares.astype(F32)
        return carry

    return step


def kernel(
    packed, widths_in, bases_in, scale_in, owner_in, key_in, bounds_in,
    means, mean_squares, share,
    words, widths, bases, scale, owner_part, key_part, bounds,
    lanes_in, keep, masks, rows, send, recv, tsend, trecv,
    word_sems, small_sems, send_sems, recv_sems, tsend_sems, trecv_sems,
):
    group, member = lax.axis_index("group"), lax.axis_index("member")

    def word_copy(t, it):
        at = pl.ds(pl.multiple_of(it * CHUNK_ROWS, CHUNK_ROWS), CHUNK_ROWS)
        return pltpu.make_async_copy(
            packed.at[at, pl.ds(t * LANES, LANES)], words.at[t, at], word_sems.at[t, it]
        )

    small = [
        pltpu.make_async_copy(source, target, small_sems.at[i])
        for i, (source, target) in enumerate(
            [
                (bounds_in, bounds),
                (widths_in, widths),
                (bases_in, bases),
                (owner_in, owner_part),
                (key_in, key_part),
                (scale_in, scale),
            ]
        )
    ]
    for copy in small:
        copy.start()
    for t in range(2):
        for it in range(CHUNKS):
            word_copy(t, it).start()

    for c in range(1, PARTS):
        for s in range(MEMBERS):
            recv[c, s * SLOTS + 8 : (s + 1) * SLOTS, :] = jnp.zeros((8, LANES), F32)

    barrier = pltpu.get_barrier_semaphore()

    def greet_member(k, carry):
        pl.semaphore_signal(
            barrier, inc=1, device_id=(group, lax.rem(member + k, MEMBERS)), device_id_type=MESH
        )
        return carry

    def greet_group(k, carry):
        pl.semaphore_signal(
            barrier, inc=1, device_id=(lax.rem(group + k, GROUPS), member), device_id_type=MESH
        )
        return carry

    lax.fori_loop(1, MEMBERS, greet_member, 0)
    lax.fori_loop(1, GROUPS, greet_group, 0)

    small[3].wait()
    small[4].wait()
    lanes_in[...] = jnp.full((8, LANES), -1, I32)
    lanes_in[0:1, 0:BLOCKS_DEV] = owner_part[...]
    lanes_in[1:2, 0:BLOCKS_DEV] = key_part[...]
    owner = lanes_in[0:1, :]
    key = lanes_in[1:2, :]
    named = iota((MEMBERS, LANES), 0) == owner
    named_f = jnp.where(named, 1.0, 0.0).astype(F32)
    before = jnp.where(iota((LANES, LANES), 0) < iota((LANES, LANES), 1), 1.0, 0.0).astype(BF16)
    rank = jnp.sum(named_f * dot(named_f.astype(BF16), before), 0, keepdims=True).astype(I32)
    target = owner * SLOTS + rank
    placer = jnp.where(
        iota((MEMBERS * SLOTS, 2 * LANES), 0) == jnp.concatenate([target, target], 1), 1.0, 0.0
    ).astype(BF16)
    meta_lane = jnp.where(
        iota((LANES, LANES), 0) == rank + lax.rem(member, 8) * SLOTS, 1.0, 0.0
    ).astype(BF16)
    weights = mask_weights()

    for copy in small[:3]:
        copy.wait()
    limits = [bounds[i] for i in range(4)]
    test = predicate(words, widths, bases, limits, keep)
    keep[BLOCKS_DEV:LANES, :] = jnp.zeros((LANES - BLOCKS_DEV, LANES), F32)

    def first_pass(it, carry):
        word_copy(0, it).wait()
        return test(it, carry)

    lax.fori_loop(0, CHUNKS, first_pass, 0)
    kept = keep[...].astype(BF16)
    masks[...] = dot(kept, weights).astype(I32)
    kept_lane = dot_nt(jnp.ones((16, LANES), BF16), kept)[0:1, :]
    meta = dot_nt(
        jnp.concatenate(
            [
                jnp.where(named, (key + 1).astype(F32), 0.0),
                jnp.where(named, jnp.broadcast_to(kept_lane, named.shape), 0.0),
            ],
            0,
        ).astype(BF16),
        meta_lane,
    )

    def message(c, k):
        other = lax.rem(member + k * STRIDE, MEMBERS)
        size = SLOTS if c == 0 else CAP
        return pltpu.make_async_remote_copy(
            src_ref=send.at[c, pl.ds(pl.multiple_of(other * SLOTS, SLOTS), size)],
            dst_ref=recv.at[c, pl.ds(pl.multiple_of(member * SLOTS, SLOTS), size)],
            send_sem=send_sems.at[c],
            recv_sem=recv_sems.at[c],
            device_id=(group, other),
            device_id_type=MESH,
        )

    def all_messages(c):
        at = pl.ds(0, (MEMBERS - 1) * (SLOTS if c == 0 else CAP))
        return pltpu.make_async_remote_copy(
            src_ref=send.at[c, at],
            dst_ref=recv.at[c, at],
            send_sem=send_sems.at[c],
            recv_sem=recv_sems.at[c],
            device_id=(group, lax.rem(member + 1, MEMBERS)),
            device_id_type=MESH,
        )

    def total(c, k):
        other = lax.rem(group + k, GROUPS)
        size = KD + 8 if c == 0 else KD
        return pltpu.make_async_remote_copy(
            src_ref=tsend.at[c, pl.ds(pl.multiple_of(other * PITCH, 8), size)],
            dst_ref=trecv.at[c, pl.ds(pl.multiple_of((k - 1) * PITCH, 8), size)],
            send_sem=tsend_sems.at[c],
            recv_sem=trecv_sems.at[c],
            device_id=(other, member),
            device_id_type=MESH,
        )

    def all_totals(c):
        at = pl.ds(0, (GROUPS - 1) * (KD + 8 if c == 0 else KD))
        return pltpu.make_async_remote_copy(
            src_ref=tsend.at[c, at],
            dst_ref=trecv.at[c, at],
            send_sem=tsend_sems.at[c],
            recv_sem=trecv_sems.at[c],
            device_id=(lax.rem(group + 1, GROUPS), member),
            device_id_type=MESH,
        )

    def start_messages(c):
        def start_one(k, carry):
            message(c, k).start()
            return carry

        lax.fori_loop(1, MEMBERS, start_one, 0)

    def start_totals(c):
        for k in (4, 3, 5, 2, 6, 1, 7):
            total(c, k).start()

    for t in range(2):
        work = block_rows(words, widths, bases, masks, rows, t)

        def second_pass(it, carry):
            if t == 1:
                word_copy(1, it).wait()
            return work(it, carry)

        lax.fori_loop(0, CHUNKS, second_pass, 0)
        high, low = split(rows[...])
        pad = jnp.zeros((LANES - BLOCKS_DEV, 2 * LANES), BF16)
        placed = dot(placer, jnp.concatenate([high, pad, low, pad], 0))
        own = pl.ds(pl.multiple_of(member * SLOTS, SLOTS), SLOTS)
        for q in range(2):
            c = 2 * t + q
            send[c] = placed[:, q * LANES : (q + 1) * LANES]
            if c == 0:
                send[0, pl.ds(14, MEMBERS, stride=SLOTS), :] = meta[0:MEMBERS, :]
                send[0, pl.ds(15, MEMBERS, stride=SLOTS), :] = meta[MEMBERS:, :]
                pl.semaphore_wait(barrier, MEMBERS - 1 + GROUPS - 1)
            start_messages(c)
            recv[c, own, :] = send[c, own, :]

    named_key = None
    for c in range(PARTS):
        all_messages(c).wait_recv()
        if c == 0:
            key_lanes, count_lanes = [], []
            for b in range(4):
                for lanes, row in ((key_lanes, 14), (count_lanes, 15)):
                    tile = recv[0, pl.ds(b * 8 * SLOTS + row, 8, stride=SLOTS), :]
                    lanes.append(jnp.sum(tile, 0, keepdims=True))
            key_lane = jnp.concatenate(key_lanes, 1).astype(I32) - 1
            count_lane = jnp.concatenate(count_lanes, 1)
            width = MEMBERS * SLOTS
            named_key = jnp.where(iota((GROUPS * KD, width), 0) == key_lane, 1.0, 0.0).astype(BF16)
            by_group = jnp.where(
                iota((16, width), 0) == (key_lane >> 5), jnp.broadcast_to(count_lane, (16, width)), 0.0
            ).astype(BF16)
            in_group = jnp.where(iota((LANES, width), 0) == (key_lane & 31), 1.0, 0.0).astype(BF16)
            counts = dot_nt(by_group, in_group)
            for g in range(GROUPS):
                tsend[0, g * PITCH + KD : (g + 1) * PITCH, :] = jnp.broadcast_to(
                    counts[g : g + 1, :], (8, LANES)
                )
        high, low = split(recv[c])
        table = dot(named_key, jnp.concatenate([high, low], 1))
        table = table[:, 0:LANES] + table[:, LANES:]
        for g in range(GROUPS):
            tsend[c, g * PITCH : g * PITCH + KD, :] = table[g * KD : (g + 1) * KD, :]
        start_totals(c)

    small[5].wait()
    at = pl.multiple_of(group * PITCH, 8)
    divisor = None
    for c in range(PARTS):
        t, q = divmod(c, 2)
        mine = tsend[c, pl.ds(at, KD), :]
        all_totals(c).wait_recv()
        for k in range(GROUPS - 1):
            mine = mine + trecv[c, k * PITCH : k * PITCH + KD, :]
        if c == 0:
            count = tsend[0, pl.ds(at + KD, 8), :]
            for k in range(GROUPS - 1):
                count = count + trecv[0, k * PITCH + KD : (k + 1) * PITCH, :]
            share[...] = count[0:1, 0:KD] * (1.0 / BLOCK)
            diagonal = iota((KD, LANES), 0) == iota((KD, LANES), 1)
            divisor = jnp.maximum(
                jnp.sum(
                    jnp.where(diagonal, jnp.broadcast_to(count[0:1, :], (KD, LANES)), 0.0),
                    1,
                    keepdims=True,
                ),
                1.0,
            )
        columns = slice(t * LANES, (t + 1) * LANES)
        by = scale[0:1, columns]
        if q == 0:
            means[:, columns] = mine * by / divisor
        else:
            mean_squares[:, columns] = mine * (by * by) / divisor

    for c in range(PARTS):
        all_messages(c).wait_send()
        all_totals(c).wait_send()


def finish(means_in, squares_in, share_in, means, squares, share, sems):
    copies = [
        pltpu.make_async_copy(source, target, sems.at[i])
        for i, (source, target) in enumerate(
            [(means_in, means), (squares_in, squares), (share_in, share)]
        )
    ]
    for copy in copies:
        copy.start()
    for copy in copies:
        copy.wait()


def shards(
    packed_words, bit_widths, column_bases, column_scale, block_owner, block_key, predicate_bounds
):
    columns = packed_words.shape[2]
    hbm = pl.BlockSpec(memory_space=pltpu.HBM)
    vmem = pl.BlockSpec(memory_space=pltpu.VMEM)
    outs = (
        jax.ShapeDtypeStruct((KD, columns), F32),
        jax.ShapeDtypeStruct((KD, columns), F32),
        jax.ShapeDtypeStruct((1, KD), F32),
    )
    results = pl.pallas_call(
        kernel,
        out_shape=tuple(pltpu.VMEM(out.shape, out.dtype) for out in outs),
        in_specs=[hbm] * 7,
        out_specs=(vmem, vmem, vmem),
        scratch_shapes=[
            pltpu.VMEM((2, BLOCKS_DEV * WORDS, LANES), I32),
            pltpu.VMEM((BLOCKS_DEV, columns), I32),
            pltpu.VMEM((BLOCKS_DEV, columns), I32),
            pltpu.VMEM((1, columns), F32),
            pltpu.VMEM((1, BLOCKS_DEV), I32),
            pltpu.VMEM((1, BLOCKS_DEV), I32),
            pltpu.SMEM((4,), I32),
            pltpu.VMEM((8, LANES), I32),
            pltpu.VMEM((LANES, LANES), F32),
            pltpu.VMEM((LANES, LANES), I32),
            pltpu.VMEM((BLOCKS_DEV, 2 * LANES), F32),
            pltpu.VMEM((PARTS, MEMBERS * SLOTS, LANES), F32),
            pltpu.VMEM((PARTS, MEMBERS * SLOTS, LANES), F32),
            pltpu.VMEM((PARTS, GROUPS * PITCH, LANES), F32),
            pltpu.VMEM((PARTS, (GROUPS - 1) * PITCH, LANES), F32),
            pltpu.SemaphoreType.DMA((2, CHUNKS)),
            pltpu.SemaphoreType.DMA((6,)),
            pltpu.SemaphoreType.DMA((PARTS,)),
            pltpu.SemaphoreType.DMA((PARTS,)),
            pltpu.SemaphoreType.DMA((PARTS,)),
            pltpu.SemaphoreType.DMA((PARTS,)),
        ],
        compiler_params=pltpu.CompilerParams(
            collective_id=0, has_side_effects=True, vmem_limit_bytes=VMEM_BYTES
        ),
        name="rollup",
    )(
        packed_words.reshape(BLOCKS_DEV * WORDS, columns),
        bit_widths,
        column_bases,
        column_scale.reshape(1, columns),
        block_owner.reshape(1, BLOCKS_DEV),
        block_key.reshape(1, BLOCKS_DEV),
        predicate_bounds,
    )
    means, mean_squares, share = pl.pallas_call(
        finish,
        out_shape=outs,
        in_specs=[vmem] * 3,
        out_specs=(hbm, hbm, hbm),
        scratch_shapes=[pltpu.SemaphoreType.DMA((3,))],
        name="finish",
    )(*[pltpu.with_memory_space_constraint(part, pltpu.VMEM) for part in results])
    return means, mean_squares, share.reshape(KD)


def solution(mesh):
    return jax.shard_map(
        shards,
        mesh=mesh,
        in_specs=(
            P(("group", "member"), None, None),
            P(("group", "member"), None),
            P(("group", "member"), None),
            P(),
            P(("group", "member"), None),
            P(("group", "member")),
            P(),
        ),
        out_specs=(
            P(("group", "member"), None),
            P(("group", "member"), None),
            P(("group", "member")),
        ),
        check_vma=False,
    )
```

```python
import functools

import jax
import jax.numpy as jnp
from jax import lax
from jax.experimental import pallas as pl
from jax.experimental.pallas import tpu as pltpu
from jax.sharding import PartitionSpec as P

BLOCK = 128
WORDS = 32
BLOCKS_DEV = 112
KD = 32
GROUPS = 8
MEMBERS = 32
LANES = 128
SLOTS = 16
CAP = 14
PARTS = 4
PITCH = KD + 8
STRIDE = 13
NEAR = (2, GROUPS - 2, 1, GROUPS - 1)
VMEM_BYTES = 60 * 1024 * 1024
UNROLL = 7
CHUNKS = BLOCKS_DEV // (8 * UNROLL)
CHUNK_ROWS = UNROLL * 256
MESH = pl.DeviceIdType.MESH
BF16 = jnp.bfloat16
F32 = jnp.float32
I32 = jnp.int32


def iota(shape, dim):
    return lax.broadcasted_iota(I32, shape, dim)


def field_place(row):
    word3 = row >> 2
    word2 = (row * 43) >> 8
    word1 = (row * 43) >> 9
    return (word1, row - 12 * word1), (word2, row - 6 * word2), (word3, row - 4 * word3)


def spread(column):
    return jnp.broadcast_to(column, (8, LANES))


def by_width(is1, is2, one, two, three):
    return jnp.where(is1, one, jnp.where(is2, two, three))


def dot(left, right):
    return lax.dot_general(left, right, (((1,), (0,)), ((), ())), preferred_element_type=F32)


def dot_nt(left, right):
    return lax.dot_general(left, right, (((1,), (1,)), ((), ())), preferred_element_type=F32)


def split(values):
    high = values.astype(BF16)
    return high, (values - high.astype(F32)).astype(BF16)


def pick(tile, lanes):
    return jnp.take_along_axis(tile, lanes, axis=1, mode="promise_in_bounds")


def predicate(words, widths, bases, bounds, keep):
    lane = iota((8, LANES), 1)
    pair = lane >> 1
    (w1, j1), (w2, j2), (w3, j3) = field_place(lane)

    def step(it, carry):
        for u in range(UNROLL):
            g = it * UNROLL + u
            width_tile = widths[pl.ds(pl.multiple_of(g * 8, 8), 8), 0:LANES]
            base_tile = bases[pl.ds(pl.multiple_of(g * 8, 8), 8), 0:LANES]
            both = words[0, pl.ds(pl.multiple_of(g * 256, 8), 8, stride=WORDS), :]
            for j in range(1, WORDS):
                tile = words[0, pl.ds(g * 256 + j, 8, stride=WORDS), :]
                both = jnp.where(pair == j, pltpu.roll(tile, 2 * j, 1), both)
            ok = None
            for c in range(2):
                w = spread(width_tile[:, c : c + 1])
                is1, is2 = w == 1, w == 2
                word = pick(both, 2 * by_width(is1, is2, w1, w2, w3) + c)
                shift = by_width(is1, is2, j1, 2 * j2, 3 * j3)
                mask = by_width(is1, is2, 1, 3, 7)
                value = ((word >> shift) & mask) + spread(base_tile[:, c : c + 1])
                inside = (value >= bounds[2 * c]) & (value <= bounds[2 * c + 1])
                ok = inside if ok is None else ok & inside
            keep[pl.ds(pl.multiple_of(g * 8, 8), 8), :] = jnp.where(ok, 1.0, 0.0).astype(F32)
        return carry

    return step


def mask_weights():
    row, lane = iota((BLOCK, LANES), 0), iota((BLOCK, LANES), 1)
    (w1, j1), (w2, j2), (w3, j3) = field_place(row)
    pair = lane & 15
    kind = lane >> 4

    def piece(word, bits):
        return jnp.where((word & 15) == pair, jnp.where(word >= 16, bits << 12, bits), 0)

    weight = jnp.where(
        kind == 0,
        piece(w3, jnp.left_shift(7, 3 * j3)),
        jnp.where(
            kind == 1,
            piece(w2, jnp.left_shift(3, 2 * j2)),
            jnp.where(kind == 2, piece(w1, jnp.left_shift(1, j1)), jnp.where(lane == 64, 1, 0)),
        ),
    )
    return weight.astype(F32).astype(BF16)


def block_rows(words, widths, bases, masks, rows, t):
    columns = slice(t * LANES, (t + 1) * LANES)
    count = lax.population_count

    def step(it, carry):
        for u in range(UNROLL):
            g = it * UNROLL + u
            at = pl.ds(pl.multiple_of(g * 8, 8), 8)
            opened = masks[at, :]
            width = widths[at, columns]
            base = bases[at, columns]
            is1, is2 = width == 1, width == 2
            a0 = by_width(is1, is2, 0xFFFFFF, 0x555555, 0o11111111)
            a1 = jnp.where(is1, 0, a0)
            a2 = jnp.where(is1 | is2, 0, a0)
            place = by_width(is1, is2, 32, 16, 0)
            c0 = c1 = c2 = c01 = c02 = c12 = jnp.zeros((8, LANES), I32)
            for i in range(16):
                low = words[t, pl.ds(g * 256 + i, 8, stride=WORDS), :]
                high = words[t, pl.ds(g * 256 + i + 16, 8, stride=WORDS), :]
                m = (low | (high << 12)) & pick(opened, place + i)
                bit0 = m & a0
                bit1 = (m >> 1) & a1
                bit2 = (m >> 2) & a2
                c0 = c0 + count(bit0)
                c1 = c1 + count(bit1)
                c2 = c2 + count(bit2)
                c01 = c01 + count(bit0 & bit1)
                c02 = c02 + count(bit0 & bit2)
                c12 = c12 + count(bit1 & bit2)
            first = c0 + 2 * c1 + 4 * c2
            second = c0 + 4 * (c1 + c01) + 8 * c02 + 16 * (c2 + c12)
            kept = spread(opened[:, 64:65])
            total = base * kept + first
            squares = base * (total + first) + second
            rows[at, 0:LANES] = total.astype(F32)
            rows[at, LANES : 2 * LANES] = squares.astype(F32)
        return carry

    return step


def kernel(
    packed, widths_in, bases_in, scale_in, owner_in, key_in, bounds_in,
    means, mean_squares, share,
    words, widths, bases, scale, owner_part, key_part, bounds,
    lanes_in, keep, masks, rows, send, recv, tsend, trelay, tmerged, trecv, tall,
    word_sems, small_sems, send_sems, recv_sems, tsend_sems, trelay_sems, trecv_sems,
):
    group, member = lax.axis_index("group"), lax.axis_index("member")

    def word_copy(t, it):
        at = pl.ds(pl.multiple_of(it * CHUNK_ROWS, CHUNK_ROWS), CHUNK_ROWS)
        return pltpu.make_async_copy(
            packed.at[at, pl.ds(t * LANES, LANES)], words.at[t, at], word_sems.at[t, it]
        )

    small = [
        pltpu.make_async_copy(source, target, small_sems.at[i])
        for i, (source, target) in enumerate(
            [
                (bounds_in, bounds),
                (widths_in, widths),
                (bases_in, bases),
                (owner_in, owner_part),
                (key_in, key_part),
                (scale_in, scale),
            ]
        )
    ]
    for copy in small:
        copy.start()
    for t in range(2):
        for it in range(CHUNKS):
            word_copy(t, it).start()

    for c in range(1, PARTS):
        for s in range(MEMBERS):
            recv[c, s * SLOTS + 8 : (s + 1) * SLOTS, :] = jnp.zeros((8, LANES), F32)

    barrier = pltpu.get_barrier_semaphore()

    def greet_member(k, carry):
        pl.semaphore_signal(
            barrier, inc=1, device_id=(group, lax.rem(member + k, MEMBERS)), device_id_type=MESH
        )
        return carry

    def greet_group(k, carry):
        pl.semaphore_signal(
            barrier, inc=1, device_id=(lax.rem(group + k, GROUPS), member), device_id_type=MESH
        )
        return carry

    lax.fori_loop(1, MEMBERS, greet_member, 0)
    for k in NEAR:
        greet_group(k, 0)

    small[3].wait()
    small[4].wait()
    lanes_in[...] = jnp.full((8, LANES), -1, I32)
    lanes_in[0:1, 0:BLOCKS_DEV] = owner_part[...]
    lanes_in[1:2, 0:BLOCKS_DEV] = key_part[...]
    owner = lanes_in[0:1, :]
    key = lanes_in[1:2, :]
    named = iota((MEMBERS, LANES), 0) == owner
    named_f = jnp.where(named, 1.0, 0.0).astype(F32)
    before = jnp.where(iota((LANES, LANES), 0) < iota((LANES, LANES), 1), 1.0, 0.0).astype(BF16)
    rank = jnp.sum(named_f * dot(named_f.astype(BF16), before), 0, keepdims=True).astype(I32)
    target = owner * SLOTS + rank
    placer = jnp.where(
        iota((MEMBERS * SLOTS, 2 * LANES), 0) == jnp.concatenate([target, target], 1), 1.0, 0.0
    ).astype(BF16)
    meta_lane = jnp.where(
        iota((LANES, LANES), 0) == rank + lax.rem(member, 8) * SLOTS, 1.0, 0.0
    ).astype(BF16)
    weights = mask_weights()

    for copy in small[:3]:
        copy.wait()
    limits = [bounds[i] for i in range(4)]
    test = predicate(words, widths, bases, limits, keep)
    keep[BLOCKS_DEV:LANES, :] = jnp.zeros((LANES - BLOCKS_DEV, LANES), F32)

    def first_pass(it, carry):
        word_copy(0, it).wait()
        return test(it, carry)

    lax.fori_loop(0, CHUNKS, first_pass, 0)
    kept = keep[...].astype(BF16)
    masks[...] = dot(kept, weights).astype(I32)
    kept_lane = dot_nt(jnp.ones((16, LANES), BF16), kept)[0:1, :]
    meta = dot_nt(
        jnp.concatenate(
            [
                jnp.where(named, (key + 1).astype(F32), 0.0),
                jnp.where(named, jnp.broadcast_to(kept_lane, named.shape), 0.0),
            ],
            0,
        ).astype(BF16),
        meta_lane,
    )

    def message(c, k):
        other = lax.rem(member + k * STRIDE, MEMBERS)
        size = SLOTS if c == 0 else CAP
        return pltpu.make_async_remote_copy(
            src_ref=send.at[c, pl.ds(pl.multiple_of(other * SLOTS, SLOTS), size)],
            dst_ref=recv.at[c, pl.ds(pl.multiple_of(member * SLOTS, SLOTS), size)],
            send_sem=send_sems.at[c],
            recv_sem=recv_sems.at[c],
            device_id=(group, other),
            device_id_type=MESH,
        )

    def all_messages(c):
        at = pl.ds(0, (MEMBERS - 1) * (SLOTS if c == 0 else CAP))
        return pltpu.make_async_remote_copy(
            src_ref=send.at[c, at],
            dst_ref=recv.at[c, at],
            send_sem=send_sems.at[c],
            recv_sem=recv_sems.at[c],
            device_id=(group, lax.rem(member + 1, MEMBERS)),
            device_id_type=MESH,
        )

    def table_at(k):
        return pl.multiple_of(lax.rem(group + k, GROUPS) * PITCH, 8)

    def rows_of(c):
        return KD + 8 if c == 0 else KD

    def to_group(source, target, send_sem, recv_sem, k):
        return pltpu.make_async_remote_copy(
            src_ref=source,
            dst_ref=target,
            send_sem=send_sem,
            recv_sem=recv_sem,
            device_id=(lax.rem(group + k, GROUPS), member),
            device_id_type=MESH,
        )

    def far_copies(c):
        size = rows_of(c)
        side = 1 if c % 2 else -1
        hops = [(2, 4 * side, 2 * side), (0, -3, -1), (1, 3, 1)]
        return [
            to_group(
                tsend.at[c, pl.ds(table_at(GROUPS + whose), size)],
                trelay.at[c, pl.ds(slot * PITCH, size)],
                tsend_sems.at[c],
                trelay_sems.at[c],
                GROUPS + via,
            )
            for slot, whose, via in hops
        ]

    def near_copies(c):
        size = rows_of(c)
        return [
            to_group(
                tsend.at[c, pl.ds(table_at(k), size)],
                trecv.at[c, pl.ds(slot * PITCH, size)],
                tsend_sems.at[c],
                trecv_sems.at[c],
                k,
            )
            for slot, k in ((0, GROUPS - 1), (1, 1))
        ]

    def relayed_copies(c):
        size = rows_of(c)
        return [
            to_group(
                tmerged.at[c, pl.ds(slot * PITCH, size)],
                trecv.at[c, pl.ds((2 + slot) * PITCH, size)],
                tsend_sems.at[c],
                trecv_sems.at[c],
                k,
            )
            for slot, k in ((0, GROUPS - 2), (1, 2))
        ]

    def wait_for(c, sem, target, copies):
        at = pl.ds(0, copies * rows_of(c))
        to_group(tall.at[at], target.at[c, at], tsend_sems.at[c], sem, 1).wait_recv()

    def relay(c):
        size = rows_of(c)
        wait_for(c, trelay_sems.at[c], trelay, 3)
        for slot, k in ((0, GROUPS - 2), (1, 2)):
            part = tsend[c, pl.ds(table_at(k), size), :] + trelay[c, slot * PITCH : slot * PITCH + size, :]
            if slot == c % 2:
                part = part + trelay[c, 2 * PITCH : 2 * PITCH + size, :]
            tmerged[c, slot * PITCH : slot * PITCH + size, :] = part
        for copy in relayed_copies(c):
            copy.start()

    def start_messages(c):
        def start_one(k, carry):
            message(c, k).start()
            return carry

        lax.fori_loop(1, MEMBERS, start_one, 0)

    for t in range(2):
        work = block_rows(words, widths, bases, masks, rows, t)

        def second_pass(it, carry):
            if t == 1:
                word_copy(1, it).wait()
            return work(it, carry)

        lax.fori_loop(0, CHUNKS, second_pass, 0)
        high, low = split(rows[...])
        pad = jnp.zeros((LANES - BLOCKS_DEV, 2 * LANES), BF16)
        placed = dot(placer, jnp.concatenate([high, pad, low, pad], 0))
        own = pl.ds(pl.multiple_of(member * SLOTS, SLOTS), SLOTS)
        for q in range(2):
            c = 2 * t + q
            send[c] = placed[:, q * LANES : (q + 1) * LANES]
            if c == 0:
                send[0, pl.ds(14, MEMBERS, stride=SLOTS), :] = meta[0:MEMBERS, :]
                send[0, pl.ds(15, MEMBERS, stride=SLOTS), :] = meta[MEMBERS:, :]
                pl.semaphore_wait(barrier, MEMBERS - 1 + len(NEAR))
            start_messages(c)
            recv[c, own, :] = send[c, own, :]

    named_key = None
    for c in range(PARTS):
        all_messages(c).wait_recv()
        if c == 0:
            key_lanes, count_lanes = [], []
            for b in range(4):
                for lanes, row in ((key_lanes, 14), (count_lanes, 15)):
                    tile = recv[0, pl.ds(b * 8 * SLOTS + row, 8, stride=SLOTS), :]
                    lanes.append(jnp.sum(tile, 0, keepdims=True))
            key_lane = jnp.concatenate(key_lanes, 1).astype(I32) - 1
            count_lane = jnp.concatenate(count_lanes, 1)
            width = MEMBERS * SLOTS
            named_key = jnp.where(iota((GROUPS * KD, width), 0) == key_lane, 1.0, 0.0).astype(BF16)
            by_group = jnp.where(
                iota((16, width), 0) == (key_lane >> 5), jnp.broadcast_to(count_lane, (16, width)), 0.0
            ).astype(BF16)
            in_group = jnp.where(iota((LANES, width), 0) == (key_lane & 31), 1.0, 0.0).astype(BF16)
            counts = dot_nt(by_group, in_group)
            for g in range(GROUPS):
                tsend[0, g * PITCH + KD : (g + 1) * PITCH, :] = jnp.broadcast_to(
                    counts[g : g + 1, :], (8, LANES)
                )
        high, low = split(recv[c])
        table = dot(named_key, jnp.concatenate([high, low], 1))
        table = table[:, 0:LANES] + table[:, LANES:]
        for g in range(GROUPS):
            tsend[c, g * PITCH : g * PITCH + KD, :] = table[g * KD : (g + 1) * KD, :]
        for copy in far_copies(c) + near_copies(c):
            copy.start()
        if c > 0:
            relay(c - 1)
    relay(PARTS - 1)

    small[5].wait()
    at = pl.multiple_of(group * PITCH, 8)
    divisor = None
    for c in range(PARTS):
        t, q = divmod(c, 2)
        mine = tsend[c, pl.ds(at, KD), :]
        wait_for(c, trecv_sems.at[c], trecv, 4)
        for k in range(4):
            mine = mine + trecv[c, k * PITCH : k * PITCH + KD, :]
        if c == 0:
            count = tsend[0, pl.ds(at + KD, 8), :]
            for k in range(4):
                count = count + trecv[0, k * PITCH + KD : (k + 1) * PITCH, :]
            share[...] = count[0:1, 0:KD] * (1.0 / BLOCK)
            diagonal = iota((KD, LANES), 0) == iota((KD, LANES), 1)
            divisor = jnp.maximum(
                jnp.sum(
                    jnp.where(diagonal, jnp.broadcast_to(count[0:1, :], (KD, LANES)), 0.0),
                    1,
                    keepdims=True,
                ),
                1.0,
            )
        columns = slice(t * LANES, (t + 1) * LANES)
        by = scale[0:1, columns]
        if q == 0:
            means[:, columns] = mine * by / divisor
        else:
            mean_squares[:, columns] = mine * (by * by) / divisor

    for c in range(PARTS):
        all_messages(c).wait_send()
        at = pl.ds(0, 7 * rows_of(c))
        to_group(
            tall.at[at], tall.at[at], tsend_sems.at[c], trecv_sems.at[c], 1
        ).wait_send()


def finish(means_in, squares_in, share_in, means, squares, share, sems):
    copies = [
        pltpu.make_async_copy(source, target, sems.at[i])
        for i, (source, target) in enumerate(
            [(means_in, means), (squares_in, squares), (share_in, share)]
        )
    ]
    for copy in copies:
        copy.start()
    for copy in copies:
        copy.wait()


def shards(
    packed_words, bit_widths, column_bases, column_scale, block_owner, block_key, predicate_bounds
):
    columns = packed_words.shape[2]
    hbm = pl.BlockSpec(memory_space=pltpu.HBM)
    vmem = pl.BlockSpec(memory_space=pltpu.VMEM)
    outs = (
        jax.ShapeDtypeStruct((KD, columns), F32),
        jax.ShapeDtypeStruct((KD, columns), F32),
        jax.ShapeDtypeStruct((1, KD), F32),
    )
    results = pl.pallas_call(
        kernel,
        out_shape=tuple(pltpu.VMEM(out.shape, out.dtype) for out in outs),
        in_specs=[hbm] * 7,
        out_specs=(vmem, vmem, vmem),
        scratch_shapes=[
            pltpu.VMEM((2, BLOCKS_DEV * WORDS, LANES), I32),
            pltpu.VMEM((BLOCKS_DEV, columns), I32),
            pltpu.VMEM((BLOCKS_DEV, columns), I32),
            pltpu.VMEM((1, columns), F32),
            pltpu.VMEM((1, BLOCKS_DEV), I32),
            pltpu.VMEM((1, BLOCKS_DEV), I32),
            pltpu.SMEM((4,), I32),
            pltpu.VMEM((8, LANES), I32),
            pltpu.VMEM((LANES, LANES), F32),
            pltpu.VMEM((LANES, LANES), I32),
            pltpu.VMEM((BLOCKS_DEV, 2 * LANES), F32),
            pltpu.VMEM((PARTS, MEMBERS * SLOTS, LANES), F32),
            pltpu.VMEM((PARTS, MEMBERS * SLOTS, LANES), F32),
            pltpu.VMEM((PARTS, GROUPS * PITCH, LANES), F32),
            pltpu.VMEM((PARTS, 3 * PITCH, LANES), F32),
            pltpu.VMEM((PARTS, 2 * PITCH, LANES), F32),
            pltpu.VMEM((PARTS, 4 * PITCH, LANES), F32),
            pltpu.VMEM((7 * PITCH, LANES), F32),
            pltpu.SemaphoreType.DMA((2, CHUNKS)),
            pltpu.SemaphoreType.DMA((6,)),
            pltpu.SemaphoreType.DMA((PARTS,)),
            pltpu.SemaphoreType.DMA((PARTS,)),
            pltpu.SemaphoreType.DMA((PARTS,)),
            pltpu.SemaphoreType.DMA((PARTS,)),
            pltpu.SemaphoreType.DMA((PARTS,)),
        ],
        compiler_params=pltpu.CompilerParams(
            collective_id=0, has_side_effects=True, vmem_limit_bytes=VMEM_BYTES
        ),
        name="rollup",
    )(
        packed_words.reshape(BLOCKS_DEV * WORDS, columns),
        bit_widths,
        column_bases,
        column_scale.reshape(1, columns),
        block_owner.reshape(1, BLOCKS_DEV),
        block_key.reshape(1, BLOCKS_DEV),
        predicate_bounds,
    )
    means, mean_squares, share = pl.pallas_call(
        finish,
        out_shape=outs,
        in_specs=[vmem] * 3,
        out_specs=(hbm, hbm, hbm),
        scratch_shapes=[pltpu.SemaphoreType.DMA((3,))],
        name="finish",
    )(*[pltpu.with_memory_space_constraint(part, pltpu.VMEM) for part in results])
    return means, mean_squares, share.reshape(KD)


def solution(mesh):
    return jax.shard_map(
        shards,
        mesh=mesh,
        in_specs=(
            P(("group", "member"), None, None),
            P(("group", "member"), None),
            P(("group", "member"), None),
            P(),
            P(("group", "member"), None),
            P(("group", "member")),
            P(),
        ),
        out_specs=(
            P(("group", "member"), None),
            P(("group", "member"), None),
            P(("group", "member")),
        ),
        check_vma=False,
    )
```

```python
import functools

import jax
import jax.numpy as jnp
from jax import lax
from jax.experimental import pallas as pl
from jax.experimental.pallas import tpu as pltpu
from jax.sharding import PartitionSpec as P

BLOCK = 128
WORDS = 32
BLOCKS_DEV = 112
KD = 32
GROUPS = 8
MEMBERS = 32
LANES = 128
SLOTS = 16
CAP = 14
PARTS = 4
PITCH = KD + 8
STRIDE = 13
NEAR = (2, GROUPS - 2, 1, GROUPS - 1)
VMEM_BYTES = 60 * 1024 * 1024
UNROLL = 14
CHUNKS = BLOCKS_DEV // (8 * UNROLL)
CHUNK_ROWS = UNROLL * 256
MESH = pl.DeviceIdType.MESH
BF16 = jnp.bfloat16
F32 = jnp.float32
I32 = jnp.int32


def iota(shape, dim):
    return lax.broadcasted_iota(I32, shape, dim)


def field_place(row):
    word3 = row >> 2
    word2 = (row * 43) >> 8
    word1 = (row * 43) >> 9
    return (word1, row - 12 * word1), (word2, row - 6 * word2), (word3, row - 4 * word3)


def spread(column):
    return jnp.broadcast_to(column, (8, LANES))


def by_width(is1, is2, one, two, three):
    return jnp.where(is1, one, jnp.where(is2, two, three))


def dot(left, right):
    return lax.dot_general(left, right, (((1,), (0,)), ((), ())), preferred_element_type=F32)


def dot_nt(left, right):
    return lax.dot_general(left, right, (((1,), (1,)), ((), ())), preferred_element_type=F32)


def split(values):
    high = values.astype(BF16)
    return high, (values - high.astype(F32)).astype(BF16)


def pick(tile, lanes):
    return jnp.take_along_axis(tile, lanes, axis=1, mode="promise_in_bounds")


def predicate(words, widths, bases, bounds, keep):
    lane = iota((8, LANES), 1)
    pair = lane >> 1
    (w1, j1), (w2, j2), (w3, j3) = field_place(lane)

    def step(it, carry):
        for u in range(UNROLL):
            g = it * UNROLL + u
            width_tile = widths[pl.ds(pl.multiple_of(g * 8, 8), 8), 0:LANES]
            base_tile = bases[pl.ds(pl.multiple_of(g * 8, 8), 8), 0:LANES]
            both = words[0, pl.ds(pl.multiple_of(g * 256, 8), 8, stride=WORDS), :]
            for j in range(1, WORDS):
                tile = words[0, pl.ds(g * 256 + j, 8, stride=WORDS), :]
                both = jnp.where(pair == j, pltpu.roll(tile, 2 * j, 1), both)
            ok = None
            for c in range(2):
                w = spread(width_tile[:, c : c + 1])
                is1, is2 = w == 1, w == 2
                word = pick(both, 2 * by_width(is1, is2, w1, w2, w3) + c)
                shift = by_width(is1, is2, j1, 2 * j2, 3 * j3)
                mask = by_width(is1, is2, 1, 3, 7)
                value = ((word >> shift) & mask) + spread(base_tile[:, c : c + 1])
                inside = (value >= bounds[2 * c]) & (value <= bounds[2 * c + 1])
                ok = inside if ok is None else ok & inside
            keep[pl.ds(pl.multiple_of(g * 8, 8), 8), :] = jnp.where(ok, 1.0, 0.0).astype(F32)
        return carry

    return step


def mask_weights():
    row, lane = iota((BLOCK, LANES), 0), iota((BLOCK, LANES), 1)
    (w1, j1), (w2, j2), (w3, j3) = field_place(row)
    pair = lane & 15
    kind = lane >> 4

    def piece(word, bits):
        return jnp.where((word & 15) == pair, jnp.where(word >= 16, bits << 12, bits), 0)

    weight = jnp.where(
        kind == 0,
        piece(w3, jnp.left_shift(7, 3 * j3)),
        jnp.where(
            kind == 1,
            piece(w2, jnp.left_shift(3, 2 * j2)),
            jnp.where(kind == 2, piece(w1, jnp.left_shift(1, j1)), jnp.where(lane == 64, 1, 0)),
        ),
    )
    return weight.astype(F32).astype(BF16)


def block_rows(words, widths, bases, masks, rows, t):
    columns = slice(t * LANES, (t + 1) * LANES)
    count = lax.population_count

    def step(it, carry):
        for u in range(UNROLL):
            g = it * UNROLL + u
            at = pl.ds(pl.multiple_of(g * 8, 8), 8)
            opened = masks[at, :]
            width = widths[at, columns]
            base = bases[at, columns]
            is1, is2 = width == 1, width == 2
            a0 = by_width(is1, is2, 0xFFFFFF, 0x555555, 0o11111111)
            a1 = jnp.where(is1, 0, a0)
            a2 = jnp.where(is1 | is2, 0, a0)
            place = by_width(is1, is2, 32, 16, 0)
            c0 = c1 = c2 = c01 = c02 = c12 = jnp.zeros((8, LANES), I32)
            for i in range(16):
                low = words[t, pl.ds(g * 256 + i, 8, stride=WORDS), :]
                high = words[t, pl.ds(g * 256 + i + 16, 8, stride=WORDS), :]
                m = (low | (high << 12)) & pick(opened, place + i)
                bit0 = m & a0
                bit1 = (m >> 1) & a1
                bit2 = (m >> 2) & a2
                c0 = c0 + count(bit0)
                c1 = c1 + count(bit1)
                c2 = c2 + count(bit2)
                c01 = c01 + count(bit0 & bit1)
                c02 = c02 + count(bit0 & bit2)
                c12 = c12 + count(bit1 & bit2)
            first = c0 + 2 * c1 + 4 * c2
            second = c0 + 4 * (c1 + c01) + 8 * c02 + 16 * (c2 + c12)
            kept = spread(opened[:, 64:65])
            total = base * kept + first
            squares = base * (total + first) + second
            rows[at, 0:LANES] = total.astype(F32)
            rows[at, LANES : 2 * LANES] = squares.astype(F32)
        return carry

    return step


def kernel(
    packed, widths_in, bases_in, scale_in, owner_in, key_in, bounds_in,
    means, mean_squares, share,
    words, widths, bases, scale, owner_part, key_part, bounds,
    lanes_in, keep, masks, rows, send, recv, tsend, trelay, tmerged, trecv, tall,
    word_sems, small_sems, send_sems, recv_sems, tsend_sems, trelay_sems, trecv_sems,
):
    group, member = lax.axis_index("group"), lax.axis_index("member")

    def word_copy(t, it):
        at = pl.ds(pl.multiple_of(it * CHUNK_ROWS, CHUNK_ROWS), CHUNK_ROWS)
        return pltpu.make_async_copy(
            packed.at[at, pl.ds(t * LANES, LANES)], words.at[t, at], word_sems.at[t, it]
        )

    small = [
        pltpu.make_async_copy(source, target, small_sems.at[i])
        for i, (source, target) in enumerate(
            [
                (bounds_in, bounds),
                (widths_in, widths),
                (bases_in, bases),
                (owner_in, owner_part),
                (key_in, key_part),
                (scale_in, scale),
            ]
        )
    ]
    for copy in small:
        copy.start()
    for t in range(2):
        for it in range(CHUNKS):
            word_copy(t, it).start()

    for c in range(1, PARTS):
        for s in range(MEMBERS):
            recv[c, s * SLOTS + 8 : (s + 1) * SLOTS, :] = jnp.zeros((8, LANES), F32)

    barrier = pltpu.get_barrier_semaphore()

    def greet_member(k, carry):
        pl.semaphore_signal(
            barrier, inc=1, device_id=(group, lax.rem(member + k, MEMBERS)), device_id_type=MESH
        )
        return carry

    def greet_group(k, carry):
        pl.semaphore_signal(
            barrier, inc=1, device_id=(lax.rem(group + k, GROUPS), member), device_id_type=MESH
        )
        return carry

    lax.fori_loop(1, MEMBERS, greet_member, 0)
    for k in NEAR:
        greet_group(k, 0)

    small[3].wait()
    small[4].wait()
    lanes_in[...] = jnp.full((8, LANES), -1, I32)
    lanes_in[0:1, 0:BLOCKS_DEV] = owner_part[...]
    lanes_in[1:2, 0:BLOCKS_DEV] = key_part[...]
    owner = lanes_in[0:1, :]
    key = lanes_in[1:2, :]
    named = iota((MEMBERS, LANES), 0) == owner
    named_f = jnp.where(named, 1.0, 0.0).astype(F32)
    before = jnp.where(iota((LANES, LANES), 0) < iota((LANES, LANES), 1), 1.0, 0.0).astype(BF16)
    rank = jnp.sum(named_f * dot(named_f.astype(BF16), before), 0, keepdims=True).astype(I32)
    target = owner * SLOTS + rank
    placer = jnp.where(
        iota((MEMBERS * SLOTS, 2 * LANES), 0) == jnp.concatenate([target, target], 1), 1.0, 0.0
    ).astype(BF16)
    meta_lane = jnp.where(
        iota((LANES, LANES), 0) == rank + lax.rem(member, 8) * SLOTS, 1.0, 0.0
    ).astype(BF16)
    weights = mask_weights()

    for copy in small[:3]:
        copy.wait()
    limits = [bounds[i] for i in range(4)]
    test = predicate(words, widths, bases, limits, keep)
    keep[BLOCKS_DEV:LANES, :] = jnp.zeros((LANES - BLOCKS_DEV, LANES), F32)

    def first_pass(it, carry):
        word_copy(0, it).wait()
        return test(it, carry)

    lax.fori_loop(0, CHUNKS, first_pass, 0)
    kept = keep[...].astype(BF16)
    masks[...] = dot(kept, weights).astype(I32)
    kept_lane = dot_nt(jnp.ones((16, LANES), BF16), kept)[0:1, :]
    meta = dot_nt(
        jnp.concatenate(
            [
                jnp.where(named, (key + 1).astype(F32), 0.0),
                jnp.where(named, jnp.broadcast_to(kept_lane, named.shape), 0.0),
            ],
            0,
        ).astype(BF16),
        meta_lane,
    )

    def message(c, k):
        other = lax.rem(member + k * STRIDE, MEMBERS)
        size = SLOTS if c == 0 else CAP
        return pltpu.make_async_remote_copy(
            src_ref=send.at[c, pl.ds(pl.multiple_of(other * SLOTS, SLOTS), size)],
            dst_ref=recv.at[c, pl.ds(pl.multiple_of(member * SLOTS, SLOTS), size)],
            send_sem=send_sems.at[c],
            recv_sem=recv_sems.at[c],
            device_id=(group, other),
            device_id_type=MESH,
        )

    def all_messages(c):
        at = pl.ds(0, (MEMBERS - 1) * (SLOTS if c == 0 else CAP))
        return pltpu.make_async_remote_copy(
            src_ref=send.at[c, at],
            dst_ref=recv.at[c, at],
            send_sem=send_sems.at[c],
            recv_sem=recv_sems.at[c],
            device_id=(group, lax.rem(member + 1, MEMBERS)),
            device_id_type=MESH,
        )

    def table_at(k):
        return pl.multiple_of(lax.rem(group + k, GROUPS) * PITCH, 8)

    def rows_of(c):
        return KD + 8 if c == 0 else KD

    def to_group(source, target, send_sem, recv_sem, k):
        return pltpu.make_async_remote_copy(
            src_ref=source,
            dst_ref=target,
            send_sem=send_sem,
            recv_sem=recv_sem,
            device_id=(lax.rem(group + k, GROUPS), member),
            device_id_type=MESH,
        )

    def far_copies(c):
        size = rows_of(c)
        side = 1 if c % 2 else -1
        hops = [(2, 4 * side, 2 * side), (0, -3, -1), (1, 3, 1)]
        return [
            to_group(
                tsend.at[c, pl.ds(table_at(GROUPS + whose), size)],
                trelay.at[c, pl.ds(slot * PITCH, size)],
                tsend_sems.at[c],
                trelay_sems.at[c],
                GROUPS + via,
            )
            for slot, whose, via in hops
        ]

    def near_copies(c):
        size = rows_of(c)
        return [
            to_group(
                tsend.at[c, pl.ds(table_at(k), size)],
                trecv.at[c, pl.ds(slot * PITCH, size)],
                tsend_sems.at[c],
                trecv_sems.at[c],
                k,
            )
            for slot, k in ((0, GROUPS - 1), (1, 1))
        ]

    def relayed_copies(c):
        size = rows_of(c)
        return [
            to_group(
                tmerged.at[c, pl.ds(slot * PITCH, size)],
                trecv.at[c, pl.ds((2 + slot) * PITCH, size)],
                tsend_sems.at[c],
                trecv_sems.at[c],
                k,
            )
            for slot, k in ((0, GROUPS - 2), (1, 2))
        ]

    def wait_for(c, sem, target, copies):
        at = pl.ds(0, copies * rows_of(c))
        to_group(tall.at[at], target.at[c, at], tsend_sems.at[c], sem, 1).wait_recv()

    def relay(c):
        size = rows_of(c)
        wait_for(c, trelay_sems.at[c], trelay, 3)
        for slot, k in ((0, GROUPS - 2), (1, 2)):
            part = tsend[c, pl.ds(table_at(k), size), :] + trelay[c, slot * PITCH : slot * PITCH + size, :]
            if slot == c % 2:
                part = part + trelay[c, 2 * PITCH : 2 * PITCH + size, :]
            tmerged[c, slot * PITCH : slot * PITCH + size, :] = part
        for copy in relayed_copies(c):
            copy.start()

    def start_messages(c):
        def start_one(k, carry):
            message(c, k).start()
            return carry

        lax.fori_loop(1, MEMBERS, start_one, 0)

    for t in range(2):
        work = block_rows(words, widths, bases, masks, rows, t)

        def second_pass(it, carry):
            if t == 1:
                word_copy(1, it).wait()
            return work(it, carry)

        lax.fori_loop(0, CHUNKS, second_pass, 0)
        high, low = split(rows[...])
        pad = jnp.zeros((LANES - BLOCKS_DEV, 2 * LANES), BF16)
        placed = dot(placer, jnp.concatenate([high, pad, low, pad], 0))
        own = pl.ds(pl.multiple_of(member * SLOTS, SLOTS), SLOTS)
        for q in range(2):
            c = 2 * t + q
            send[c] = placed[:, q * LANES : (q + 1) * LANES]
            if c == 0:
                send[0, pl.ds(14, MEMBERS, stride=SLOTS), :] = meta[0:MEMBERS, :]
                send[0, pl.ds(15, MEMBERS, stride=SLOTS), :] = meta[MEMBERS:, :]
                pl.semaphore_wait(barrier, MEMBERS - 1 + len(NEAR))
            if c < 3:
                start_messages(c)
            recv[c, own, :] = send[c, own, :]

    named_key = None
    for c in range(PARTS):
        all_messages(c).wait_recv()
        if c == 0:
            key_lanes, count_lanes = [], []
            for b in range(4):
                for lanes, row in ((key_lanes, 14), (count_lanes, 15)):
                    tile = recv[0, pl.ds(b * 8 * SLOTS + row, 8, stride=SLOTS), :]
                    lanes.append(jnp.sum(tile, 0, keepdims=True))
            key_lane = jnp.concatenate(key_lanes, 1).astype(I32) - 1
            count_lane = jnp.concatenate(count_lanes, 1)
            width = MEMBERS * SLOTS
            named_key = jnp.where(iota((GROUPS * KD, width), 0) == key_lane, 1.0, 0.0).astype(BF16)
            by_group = jnp.where(
                iota((16, width), 0) == (key_lane >> 5), jnp.broadcast_to(count_lane, (16, width)), 0.0
            ).astype(BF16)
            in_group = jnp.where(iota((LANES, width), 0) == (key_lane & 31), 1.0, 0.0).astype(BF16)
            counts = dot_nt(by_group, in_group)
            for g in range(GROUPS):
                tsend[0, g * PITCH + KD : (g + 1) * PITCH, :] = jnp.broadcast_to(
                    counts[g : g + 1, :], (8, LANES)
                )
        high, low = split(recv[c])
        table = dot(named_key, jnp.concatenate([high, low], 1))
        table = table[:, 0:LANES] + table[:, LANES:]
        for g in range(GROUPS):
            tsend[c, g * PITCH : g * PITCH + KD, :] = table[g * KD : (g + 1) * KD, :]
        for copy in far_copies(c) + near_copies(c):
            copy.start()
        if c == 0:
            start_messages(3)
        if c > 0:
            relay(c - 1)
    relay(PARTS - 1)

    small[5].wait()
    at = pl.multiple_of(group * PITCH, 8)
    divisor = None
    for c in range(PARTS):
        t, q = divmod(c, 2)
        mine = tsend[c, pl.ds(at, KD), :]
        wait_for(c, trecv_sems.at[c], trecv, 4)
        for k in range(4):
            mine = mine + trecv[c, k * PITCH : k * PITCH + KD, :]
        if c == 0:
            count = tsend[0, pl.ds(at + KD, 8), :]
            for k in range(4):
                count = count + trecv[0, k * PITCH + KD : (k + 1) * PITCH, :]
            share[...] = count[0:1, 0:KD] * (1.0 / BLOCK)
            diagonal = iota((KD, LANES), 0) == iota((KD, LANES), 1)
            divisor = jnp.maximum(
                jnp.sum(
                    jnp.where(diagonal, jnp.broadcast_to(count[0:1, :], (KD, LANES)), 0.0),
                    1,
                    keepdims=True,
                ),
                1.0,
            )
        columns = slice(t * LANES, (t + 1) * LANES)
        by = scale[0:1, columns]
        if q == 0:
            means[:, columns] = mine * by / divisor
        else:
            mean_squares[:, columns] = mine * (by * by) / divisor

    for c in range(PARTS):
        all_messages(c).wait_send()
        at = pl.ds(0, 7 * rows_of(c))
        to_group(
            tall.at[at], tall.at[at], tsend_sems.at[c], trecv_sems.at[c], 1
        ).wait_send()


def finish(means_in, squares_in, share_in, means, squares, share, sems):
    copies = [
        pltpu.make_async_copy(source, target, sems.at[i])
        for i, (source, target) in enumerate(
            [(means_in, means), (squares_in, squares), (share_in, share)]
        )
    ]
    for copy in copies:
        copy.start()
    for copy in copies:
        copy.wait()


def shards(
    packed_words, bit_widths, column_bases, column_scale, block_owner, block_key, predicate_bounds
):
    columns = packed_words.shape[2]
    hbm = pl.BlockSpec(memory_space=pltpu.HBM)
    vmem = pl.BlockSpec(memory_space=pltpu.VMEM)
    outs = (
        jax.ShapeDtypeStruct((KD, columns), F32),
        jax.ShapeDtypeStruct((KD, columns), F32),
        jax.ShapeDtypeStruct((1, KD), F32),
    )
    results = pl.pallas_call(
        kernel,
        out_shape=tuple(pltpu.VMEM(out.shape, out.dtype) for out in outs),
        in_specs=[hbm] * 7,
        out_specs=(vmem, vmem, vmem),
        scratch_shapes=[
            pltpu.VMEM((2, BLOCKS_DEV * WORDS, LANES), I32),
            pltpu.VMEM((BLOCKS_DEV, columns), I32),
            pltpu.VMEM((BLOCKS_DEV, columns), I32),
            pltpu.VMEM((1, columns), F32),
            pltpu.VMEM((1, BLOCKS_DEV), I32),
            pltpu.VMEM((1, BLOCKS_DEV), I32),
            pltpu.SMEM((4,), I32),
            pltpu.VMEM((8, LANES), I32),
            pltpu.VMEM((LANES, LANES), F32),
            pltpu.VMEM((LANES, LANES), I32),
            pltpu.VMEM((BLOCKS_DEV, 2 * LANES), F32),
            pltpu.VMEM((PARTS, MEMBERS * SLOTS, LANES), F32),
            pltpu.VMEM((PARTS, MEMBERS * SLOTS, LANES), F32),
            pltpu.VMEM((PARTS, GROUPS * PITCH, LANES), F32),
            pltpu.VMEM((PARTS, 3 * PITCH, LANES), F32),
            pltpu.VMEM((PARTS, 2 * PITCH, LANES), F32),
            pltpu.VMEM((PARTS, 4 * PITCH, LANES), F32),
            pltpu.VMEM((7 * PITCH, LANES), F32),
            pltpu.SemaphoreType.DMA((2, CHUNKS)),
            pltpu.SemaphoreType.DMA((6,)),
            pltpu.SemaphoreType.DMA((PARTS,)),
            pltpu.SemaphoreType.DMA((PARTS,)),
            pltpu.SemaphoreType.DMA((PARTS,)),
            pltpu.SemaphoreType.DMA((PARTS,)),
            pltpu.SemaphoreType.DMA((PARTS,)),
        ],
        compiler_params=pltpu.CompilerParams(
            collective_id=0, has_side_effects=True, vmem_limit_bytes=VMEM_BYTES
        ),
        name="rollup",
    )(
        packed_words.reshape(BLOCKS_DEV * WORDS, columns),
        bit_widths,
        column_bases,
        column_scale.reshape(1, columns),
        block_owner.reshape(1, BLOCKS_DEV),
        block_key.reshape(1, BLOCKS_DEV),
        predicate_bounds,
    )
    means, mean_squares, share = pl.pallas_call(
        finish,
        out_shape=outs,
        in_specs=[vmem] * 3,
        out_specs=(hbm, hbm, hbm),
        scratch_shapes=[pltpu.SemaphoreType.DMA((3,))],
        name="finish",
    )(*[pltpu.with_memory_space_constraint(part, pltpu.VMEM) for part in results])
    return means, mean_squares, share.reshape(KD)


def solution(mesh):
    return jax.shard_map(
        shards,
        mesh=mesh,
        in_specs=(
            P(("group", "member"), None, None),
            P(("group", "member"), None),
            P(("group", "member"), None),
            P(),
            P(("group", "member"), None),
            P(("group", "member")),
            P(),
        ),
        out_specs=(
            P(("group", "member"), None),
            P(("group", "member"), None),
            P(("group", "member")),
        ),
        check_vma=False,
    )
```
